32 devices in a mesh: gx: 4 (over z), gy: 8 (over y, x, core).
Axes of the slice: x: 2, y: 2, z: 4, core: 2. Of those that a mesh axis runs over, the one named last changes fastest.
Arguments:
- probes: bfloat16 [3, 32, 384, 1024], P(None, None, 'gx', 'gy'), may hold values from -400 to 400
- depth: float32 [384, 1024], P('gx', 'gy'), may hold values from 0.5 to 2
- east_flow: float32 [384, 1024], P('gx', 'gy'), may hold values from -1 to 1
- north_flow: float32 [384, 1024], P('gx', 'gy'), may hold values from -1 to 1
- land_sea: int32 [384, 1024], P('gx', 'gy'), may hold values 0 or 1
Outputs:
- basis: bfloat16 [3, 32, 384, 1024], P(None, None, 'gx', 'gy')
- triangle: float32 [32, 32], replicated
The draws below stay inside these ranges and needn't reach their ends.
Inputs may be any that keep to these rules, and one draw needn't show every extreme that they name: `land_sea`: 1 marks a sea cell, 0 a land cell.
All inputs are finite; a program needn't handle non-finite values. No bound on the sum of `land_sea` on one device may be relied on, other than what follows from the above.
Results may differ from the reference program's by a relative error of at most 0.001.
Values sent between devices are 32-bit elements; how exact they have to be, the bound alone decides.
No kernel may reach another device: no remote copies, remote signals or barrier semaphores. Data moves between devices by JAX's collectives and lax.ppermute only.
A program may use at most 128 MiB of HBM per device.

```python
import math
import jax
import jax.numpy as jnp
from jax import lax

FIELDS = 3
PROBES = 32
STEPS = 2
CX = 96
NX = 384
NY = 1024


def draw_probes(key, part):
    key = jax.random.fold_in(key, 11)
    keys = jax.random.split(key, 3)
    row_scale = jnp.exp(jax.random.uniform(keys[0], (NX,), jnp.float32) * jnp.log(10.0))
    column_scale = jnp.exp(jax.random.uniform(keys[1], (NY,), jnp.float32) * jnp.log(10.0))
    position = jnp.arange(NX, dtype=jnp.float32) / (NX - 1.0) - 1.0
    trend = jnp.exp(jnp.log(3.0) * position)
    values = jax.random.truncated_normal(keys[2], -4.0, 4.0, (FIELDS, PROBES, NX, NY), jnp.float32)
    scaled = values * (row_scale * trend)[:, None] * column_scale[None, :]
    return scaled.astype(jnp.bfloat16)


def touch_ends(array, rng, least, high):
    longest = array.shape.index(max(array.shape))
    spots = []
    for shift in (0, 1):
        where = [jax.random.randint(jax.random.fold_in(rng, axis), (), 0, length) for axis, length in enumerate(array.shape)]
        where[longest] = (where[longest] + shift) % array.shape[longest]
        spots.append(tuple(where))
    return array.at[spots[0]].set(least).at[spots[1]].set(high)


def block_levels(rng, extent, pieces, low, top_value):
    loudness, own = 1.0, jax.random.fold_in(rng, 6)
    for dim, shards_of in pieces:
        draws = jnp.exp(jax.random.uniform(jax.random.fold_in(own, dim), (shards_of,), jnp.float32, low / len(pieces), top_value / len(pieces)))
        loudness = loudness * jnp.repeat(draws, extent[dim] // shards_of).reshape([-1 if axis == dim else 1 for axis in range(len(extent))])
    return loudness


def setup_inputs(seed: int = 0) -> dict:
    arg_keys = jax.random.split(jax.random.key(seed), 6)
    probes = draw_probes(jax.random.fold_in(arg_keys[5], 71), 0)
    depth = jnp.clip(jnp.exp(math.log(2.0) - 1.3862944 * jax.random.uniform(arg_keys[1], (NX, NY), jnp.float32) ** block_levels(arg_keys[1], (NX, NY), ((0, 4), (1, 8)), -0.2, 0.2)), 0.5, 2.0)
    east_flow = jnp.clip(jax.random.uniform(arg_keys[2], (NX, NY), jnp.float32, -1.0, 1.0) * block_levels(arg_keys[2], (NX, NY), ((0, 4), (1, 8)), -0.4, 0.0), -1.0, 1.0)
    north_flow = jnp.clip(jax.random.uniform(arg_keys[3], (NX, NY), jnp.float32, -1.0, 1.0) * block_levels(arg_keys[3], (NX, NY), ((0, 4), (1, 8)), -0.4, 0.0), -1.0, 1.0)
    land_sea = touch_ends((jax.random.randint(arg_keys[4], (NX, NY), 0, 5) < 4).astype(jnp.int32), jax.random.fold_in(arg_keys[4], 1), 0, 1)
    return {"probes": probes, "depth": depth, "east_flow": east_flow, "north_flow": north_flow, "land_sea": land_sea}


time_step = 0.3
coriolis = 0.5
gravity = 1.0

def slope_first(field):
    padded = jnp.pad(field, ((0, 0), (1, 1), (0, 0)))
    return 0.5 * (padded[:, 2:, :] - padded[:, :-2, :])

def slope_second(field):
    padded = jnp.pad(field, ((0, 0), (0, 0), (1, 1)))
    return 0.5 * (padded[:, :, 2:] - padded[:, :, :-2])

def advance(height, east_vel, north_vel, depth, east_flow, north_flow, sea):

    def carried(field):
        return east_flow * slope_first(field) + north_flow * slope_second(field)
    east_new = sea * (east_vel - time_step * (carried(east_vel) - coriolis * north_vel + gravity * slope_first(height)))
    north_new = sea * (north_vel - time_step * (carried(north_vel) + coriolis * east_vel + gravity * slope_second(height)))
    height_new = sea * (height - time_step * (carried(height) + slope_first(depth * east_new) + slope_second(depth * north_new)))
    return (height_new, east_new, north_new)

def evolve_block(probes, coefs, start):
    margin = 2 * STEPS
    width = CX + 2 * margin
    lowest = jnp.clip(start - margin, 0, NX - width).astype(jnp.int32)
    slab = lax.dynamic_slice_in_dim(probes, lowest, width, 2).astype(jnp.float32)
    local = lax.dynamic_slice_in_dim(coefs, lowest, width, 1)
    depth, east_flow, north_flow, sea = (local[0], local[1], local[2], local[3])
    height, east_vel, north_vel = (slab[0] * sea, slab[1] * sea, slab[2] * sea)
    for step in range(STEPS):
        height, east_vel, north_vel = advance(height, east_vel, north_vel, depth, east_flow, north_flow, sea)
    stacked = jnp.stack([height, east_vel, north_vel])
    return lax.dynamic_slice_in_dim(stacked, (start - lowest).astype(jnp.int32), CX, 2)

def reference(probes, depth, east_flow, north_flow, land_sea):
    coefs = jnp.stack([depth, east_flow, north_flow, land_sea.astype(jnp.float32)])
    starts = jnp.arange(NX // CX, dtype=jnp.int32) * CX

    def add_gram(total, start):
        block = evolve_block(probes, coefs, start)
        return (total + jnp.einsum('cpxy,cqxy->pq', block, block, precision=lax.Precision.HIGHEST), None)
    total, unused = lax.scan(add_gram, jnp.zeros((PROBES, PROBES), jnp.float32), starts)
    upper = jnp.linalg.cholesky(total).T
    inverse = lax.linalg.triangular_solve(upper, jnp.eye(PROBES, dtype=upper.dtype), left_side=True, lower=False)
    scale = math.sqrt(FIELDS * NX * NY)

    def place(index, basis):
        start = (index * CX).astype(jnp.int32)
        block = evolve_block(probes, coefs, start)
        piece = (jnp.einsum('cpxy,pq->cqxy', block, inverse, precision=lax.Precision.HIGHEST) * scale).astype(jnp.bfloat16)
        return lax.dynamic_update_slice_in_dim(basis, piece, start, 2)
    basis = lax.fori_loop(0, NX // CX, place, jnp.zeros((FIELDS, PROBES, NX, NY), jnp.bfloat16))
    return (basis, upper / scale)
```

```python
import functools
import math

import jax
import jax.numpy as jnp
from jax import lax
from jax.experimental import pallas as pl
from jax.experimental.pallas import tpu as pltpu
from jax.sharding import PartitionSpec as P

STEPS = 2
HALO = 2 * STEPS
LANES = 128
TOP = 8

time_step = 0.3
coriolis = 0.5
gravity = 1.0

VMEM_LIMIT = 56 * 1024 * 1024


def lane_ids(rows):
    return lax.broadcasted_iota(jnp.int32, (rows, LANES), 1)


def pack_kernel(probes, depth, east_flow, north_flow, land_sea, x_low, x_high, y_low, y_high):
    fields, count, rows, _ = probes.shape
    lane = lane_ids(rows)
    sea = land_sea[...].astype(jnp.float32)

    def place(index, low, high, value):
        at = HALO * index
        turned = pltpu.roll(value, at, 1)
        low = jnp.where((lane >= at) & (lane < at + HALO), turned, low)
        back = lax.rem(at - HALO + LANES, LANES)
        high = jnp.where((lane >= back) & (lane < back + HALO), turned, high)
        return low, high

    zero = jnp.zeros((rows, LANES), jnp.float32)
    for c in range(fields):

        def body(p, carry):
            value = probes[c, p].astype(jnp.float32) * sea
            x_low[c * count + p] = value[:HALO]
            x_high[c * count + p] = value[rows - HALO :]
            return place(p, *carry, value)

        low, high = lax.fori_loop(0, count, body, (zero, zero))
        y_low[c] = low
        y_high[c] = high
    low, high = zero, zero
    for a, value in enumerate((depth[...], east_flow[...], north_flow[...], sea)):
        x_low[fields * count + a] = value[:HALO]
        x_high[fields * count + a] = value[rows - HALO :]
        low, high = place(jnp.int32(a), low, high, value)
    y_low[fields] = low
    y_high[fields] = high


def pack(probes, depth, east_flow, north_flow, land_sea):
    fields, count, rows, cols = probes.shape
    x_shape = jax.ShapeDtypeStruct((fields * count + 4, HALO, cols), jnp.float32)
    y_shape = jax.ShapeDtypeStruct((fields + 1, rows, LANES), jnp.float32)
    return pl.pallas_call(
        pack_kernel,
        out_shape=(x_shape, x_shape, y_shape, y_shape),
        compiler_params=pltpu.CompilerParams(vmem_limit_bytes=VMEM_LIMIT),
        name="pack_edges",
    )(probes, depth, east_flow, north_flow, land_sea)


def evolve_kernel(
    probes, depth, east_flow, north_flow, land_sea, x_before, x_after,
    y_before, y_own_high, y_own_low, y_after, c_before, c_after,
    halves, gram, coef, strip_coef, strips, edges, state, later, flux, grid_state, total,
):
    fields, count, rows, _ = probes.shape
    own = pl.ds(TOP, rows)
    bottom = TOP + rows
    tall = rows + 2 * HALO
    first = TOP - HALO
    tiles = [(first + 8 * t, 8) for t in range(tall // 8)]
    lane8 = lane_ids(8)
    half = 0.5 * time_step

    def fold(out, at, size, values):
        deep, east, north, sea = values
        out[0, pl.ds(at, size)] = deep
        out[1, pl.ds(at, size)] = half * sea * east
        out[2, pl.ds(at, size)] = half * sea * north
        out[3, pl.ds(at, size)] = (half * gravity) * sea

    base = fields * count
    sea = land_sea[...].astype(jnp.float32)
    fold(coef, TOP, rows, (depth[...], east_flow[...], north_flow[...], sea))
    fold(coef, first, HALO, [x_before[base + a] for a in range(4)])
    fold(coef, bottom, HALO, [x_after[base + a] for a in range(4)])

    kinds = (y_before, y_own_low, y_own_high, y_after)
    back = (HALO, 0, HALO, 0)

    def gathered(tile_of, size, slot_of):
        lane = lane_ids(size)
        part = lax.rem(lane, 16) // HALO
        out = None
        for k in range(4):
            index = (HALO * slot_of(lane) + lax.rem(lane, HALO) - back[k] + LANES) & (LANES - 1)
            picked = jnp.take_along_axis(tile_of(k), index, axis=1)
            out = picked if out is None else jnp.where(part == k, picked, out)
        return out

    groups = count // 8

    def unpack(at, size, tile_of):
        values = [
            gathered(lambda k: tile_of(k, fields), size, lambda lane: jnp.full_like(lane, a))
            for a in range(4)
        ]
        fold(strip_coef, at, size, values)
        for c in range(fields):
            for g in range(groups):
                strips[0, c, g, pl.ds(at, size)] = gathered(
                    lambda k: tile_of(k, c), size, lambda lane: 8 * g + lane // 16
                )

    for t in range(rows // 8):
        unpack(TOP + 8 * t, 8, lambda k, c: kinds[k][c, pl.ds(8 * t, 8)])
    whole = jnp.zeros((8 - HALO, LANES), jnp.float32)
    unpack(0, 8, lambda k, c: jnp.concatenate([whole, c_before[k, c]], 0))
    unpack(bottom, 8, lambda k, c: jnp.concatenate([c_after[k, c], whole], 0))

    def shifted(value, wrap):
        if wrap is None:
            return pltpu.roll(value, LANES - 1, 1) - pltpu.roll(value, 1, 1)
        up = jnp.where(lane8 == 0, wrap, value)
        down = jnp.where(lane8 == LANES - 1, wrap, value)
        return pltpu.roll(up, LANES - 1, 1) - pltpu.roll(down, 1, 1)

    def velocities(source, factors, wraps, write):
        for at, size in tiles:
            here, above, below = pl.ds(at, size), pl.ds(at - 1, size), pl.ds(at + 1, size)
            deep, east, north, slope = [factors[a, here] for a in range(4)]
            h, e, n = [source(c)[here] for c in range(3)]
            xh, xe, xn = [source(c)[below] - source(c)[above] for c in range(3)]
            yh, ye, yn = [shifted(v, wraps(c, here)) for c, v in enumerate((h, e, n))]
            e_new = e + (time_step * coriolis) * n - (east * xe + north * ye + slope * xh)
            n_new = n - (time_step * coriolis) * e - (east * xn + north * yn + slope * yh)
            write(at, e_new, n_new)
            flux[0, here] = deep * e_new
            flux[1, here] = deep * n_new
            flux[2, here] = h - (east * xh + north * yh)

    def heights(factors, wraps, write, spans):
        for at, size in spans:
            here, above, below = pl.ds(at, size), pl.ds(at - 1, size), pl.ds(at + 1, size)
            along = flux[0, below] - flux[0, above]
            across = shifted(flux[1, here], wraps(here))
            write(at, flux[2, here] - factors[3, here] * (along + across))

    def keep(slot, g, at, size, value):
        edges[slot, g, pl.ds(at, size)] = jnp.where(
            lax.rem(lane_ids(size), 16) == HALO, pltpu.roll(value, LANES - 8, 1), value
        )

    def strip_body(g, carry):
        for step in range(STEPS):
            for at, size in tiles:
                for c in range(fields):
                    keep(4 * step + c, g, at, size, strips[step, c, g, pl.ds(at, size)])

            def write_velocity(at, e_new, n_new):
                if step + 1 < STEPS:
                    strips[step + 1, 1, g, pl.ds(at, 8)] = e_new
                    strips[step + 1, 2, g, pl.ds(at, 8)] = n_new

            velocities(
                lambda c: strips.at[step, c, g], strip_coef, lambda c, here: None, write_velocity
            )
            for at, size in tiles:
                keep(4 * step + 3, g, at, size, flux[1, pl.ds(at, size)])
            if step + 1 < STEPS:

                def write_height(at, h_new):
                    strips[step + 1, 0, g, pl.ds(at, 8)] = h_new

                heights(strip_coef, lambda here: None, write_height, tiles)
        return carry

    lax.fori_loop(0, groups, strip_body, 0)

    def body(p, carry):
        group = p // 8
        turn = lax.rem(2 * LANES - 16 * lax.rem(p, 8) - HALO, LANES)
        for c in range(fields):
            state[c, own] = probes[c, p].astype(jnp.float32) * land_sea[...].astype(jnp.float32)
            state[c, pl.ds(first, HALO)] = x_before[c * count + p]
            state[c, pl.ds(bottom, HALO)] = x_after[c * count + p]

        def wrap(slot):
            return lambda here: pltpu.roll(edges[slot, group, here], turn, 1)

        def row(c):
            return pl.multiple_of((c * count + p) * rows, 8)

        buffers = (state, later)
        for step in range(STEPS):
            now = buffers[step]
            last = step + 1 == STEPS

            def write_velocity(at, e_new, n_new):
                if not last:
                    later[1, pl.ds(at, 8)] = e_new
                    later[2, pl.ds(at, 8)] = n_new
                else:
                    skip, keep_to = max(TOP - at, 0), min(bottom - at, 8)
                    span = pl.ds(row(1) + (at + skip - TOP), keep_to - skip)
                    grid_state[span] = e_new[skip:keep_to]
                    span = pl.ds(row(2) + (at + skip - TOP), keep_to - skip)
                    grid_state[span] = n_new[skip:keep_to]

            velocities(
                lambda c: now.at[c], coef, lambda c, here: wrap(4 * step + c)(here), write_velocity
            )

            def write_height(at, h_new):
                if not last:
                    later[0, pl.ds(at, 8)] = h_new
                else:
                    grid_state[pl.ds(row(0) + (at - TOP), 8)] = h_new

            spans = [(TOP + 8 * t, 8) for t in range(rows // 8)] if last else tiles
            heights(coef, wrap(4 * step + 3), write_height, spans)
        return carry

    lax.fori_loop(0, count, body, 0)

    total[...] = jnp.zeros_like(total)
    for c in range(fields):

        def gram_body(i, acc):
            pair = []
            for x in range(2):
                at = c * count * rows + 2 * i + x
                pair.append(grid_state[pl.ds(at, count, stride=rows)])
            values = jnp.concatenate(pair, 1)
            top = values.astype(jnp.bfloat16)
            low = (values - top.astype(jnp.float32)).astype(jnp.bfloat16)
            both = jnp.concatenate([top, low], 0)
            halves[c * (rows // 2) + i] = both
            return acc + lax.dot_general(
                both, both, (((1,), (1,)), ((), ())), preferred_element_type=jnp.float32
            )

        acc = lax.fori_loop(
            0, rows // 2, gram_body, jnp.zeros((2 * count, 2 * count), jnp.float32), unroll=8
        )
        total[:, : 2 * count] += acc
    value = total[...]
    summed = value[:count] + value[count:]
    summed = summed + pltpu.roll(summed, LANES - count, 1)
    lane = lane_ids(count)
    summed = jnp.where(lane < count, summed, 0.0)
    out = summed[:8]
    for b in range(1, count // 8):
        out = out + pltpu.roll(summed[8 * b : 8 * b + 8], count * b, 1)
    gram[...] = out


def evolve(probes, coefs, x_before, x_after, kinds, c_before, c_after):
    fields, count, rows, cols = probes.shape
    tall = rows + 2 * TOP
    groups = count // 8
    f32 = jnp.float32
    return pl.pallas_call(
        evolve_kernel,
        out_shape=(
            jax.ShapeDtypeStruct((fields * rows // 2, 2 * count, 2 * cols), jnp.bfloat16),
            jax.ShapeDtypeStruct((8, LANES), f32),
        ),
        scratch_shapes=[
            pltpu.VMEM((4, tall, LANES), f32),
            pltpu.VMEM((4, tall, LANES), f32),
            pltpu.VMEM((STEPS, fields, groups, tall, LANES), f32),
            pltpu.VMEM((4 * STEPS, groups, tall, LANES), f32),
            pltpu.VMEM((fields, tall, LANES), f32),
            pltpu.VMEM((fields, tall, LANES), f32),
            pltpu.VMEM((3, tall, LANES), f32),
            pltpu.VMEM((fields * count * rows, LANES), f32),
            pltpu.VMEM((2 * count, LANES), f32),
        ],
        compiler_params=pltpu.CompilerParams(vmem_limit_bytes=VMEM_LIMIT),
        name="evolve_and_gram",
    )(probes, *coefs, x_before, x_after, *kinds, c_before, c_after)


def finish_kernel(scale, grams, halves, basis, triangle, grid_out):
    fields, count, rows, cols = basis.shape
    summed = jnp.sum(grams[...], 0)
    lane = lane_ids(count)
    row_id = lax.broadcasted_iota(jnp.int32, (count, LANES), 0)
    gram = jnp.concatenate(
        [summed if b == 0 else pltpu.roll(summed, LANES - count * b, 1) for b in range(count // 8)],
        0,
    )
    work = jnp.where(lane < count, gram, jnp.where(lane == row_id + count, 1.0, 0.0))
    for k in range(count):
        pivot_row = work[k : k + 1]
        ratio = work[:, k : k + 1] / work[k : k + 1, k : k + 1]
        work = work - jnp.where(row_id > k, ratio * pivot_row, 0.0)
    pivots = jnp.sum(jnp.where(lane == row_id, work, 0.0), 1, keepdims=True)
    work = work / jnp.sqrt(pivots)
    triangle[...] = jnp.where(lane >= row_id, work, 0.0)[:, :count] * (1.0 / scale)
    lower = (work * scale)[:, count : 2 * count]
    top = lower.astype(jnp.bfloat16)
    low = (lower - top.astype(jnp.float32)).astype(jnp.bfloat16)
    factor = jnp.concatenate([top, top, low], 1)

    for c in range(fields):

        def body(i, carry):
            both = halves[c * (rows // 2) + i]
            stacked = jnp.concatenate([both, both[:count]], 0)
            out = jnp.dot(factor, stacked, preferred_element_type=jnp.float32)
            for x in range(2):
                grid_out[pl.ds(2 * i + x, count, stride=rows)] = out[:, x * cols : (x + 1) * cols]
            return carry

        lax.fori_loop(0, rows // 2, body, 0, unroll=8)

        def store(q, carry):
            at = pl.multiple_of(q * rows, 8)
            basis[c, q] = grid_out[pl.ds(at, rows)].astype(jnp.bfloat16)
            return carry

        lax.fori_loop(0, count, store, 0, unroll=4)


def finish(grams, halves, shape, scale):
    fields, count, rows, cols = shape
    return pl.pallas_call(
        functools.partial(finish_kernel, scale),
        out_shape=(
            jax.ShapeDtypeStruct(shape, jnp.bfloat16),
            jax.ShapeDtypeStruct((count, count), jnp.float32),
        ),
        scratch_shapes=[pltpu.VMEM((count * rows, cols), jnp.float32)],
        compiler_params=pltpu.CompilerParams(vmem_limit_bytes=VMEM_LIMIT),
        name="factor_and_apply",
    )(grams, halves)


def per_device(probes, depth, east_flow, north_flow, land_sea):
    fields, count, rows, cols = probes.shape
    nx, ny = lax.axis_size("gx"), lax.axis_size("gy")
    up_x = [(i, i + 1) for i in range(nx - 1)]
    down_x = [(j, i) for i, j in up_x]
    up_y = [(i, i + 1) for i in range(ny - 1)]
    down_y = [(j, i) for i, j in up_y]
    coefs = (depth, east_flow, north_flow, land_sea)
    x_low, x_high, y_low, y_high = pack(probes, *coefs)
    y_before = lax.ppermute(y_high, "gy", up_y)
    y_after = lax.ppermute(y_low, "gy", down_y)
    x_before = lax.ppermute(x_high, "gx", up_x)
    x_after = lax.ppermute(x_low, "gx", down_x)
    kinds = (y_before, y_low, y_high, y_after)
    c_before = lax.ppermute(jnp.stack([k[:, rows - HALO :] for k in kinds]), "gx", up_x)
    c_after = lax.ppermute(jnp.stack([k[:, :HALO] for k in kinds]), "gx", down_x)
    halves, gram = evolve(
        probes, coefs, x_before, x_after, (y_before, y_high, y_low, y_after), c_before, c_after
    )
    devices = nx * ny
    grams = lax.all_to_all(
        jnp.broadcast_to(gram[None], (devices,) + gram.shape), ("gx", "gy"), 0, 0
    )
    scale = math.sqrt(fields * rows * nx * cols * ny)
    return finish(grams, halves, probes.shape, scale)


def solution(mesh):
    in_specs = (
        P(None, None, "gx", "gy"),
        P("gx", "gy"),
        P("gx", "gy"),
        P("gx", "gy"),
        P("gx", "gy"),
    )
    out_specs = (P(None, None, "gx", "gy"), P())
    return jax.shard_map(
        per_device, mesh=mesh, in_specs=in_specs, out_specs=out_specs, check_vma=False
    )
```

```python
import functools
import math

import jax
import jax.numpy as jnp
from jax import lax
from jax.experimental import pallas as pl
from jax.experimental.pallas import tpu as pltpu
from jax.sharding import PartitionSpec as P

STEPS = 2
HALO = 2 * STEPS
LANES = 128
TOP = 8

time_step = 0.3
coriolis = 0.5
gravity = 1.0

VMEM_LIMIT = 24 * 1024 * 1024
BLOCK = 8


def lane_ids(rows):
    return lax.broadcasted_iota(jnp.int32, (rows, LANES), 1)


def pack_kernel(
    probes, depth, east_flow, north_flow, land_sea,
    x_a, x_b, y_a, y_b, held, coefs, mask, sems,
):
    fields, count, rows, _ = held.shape
    even_x = lax.rem(lax.axis_index("gx"), 2) == 0
    even_y = lax.rem(lax.axis_index("gy"), 2) == 0
    small = [
        pltpu.make_async_copy(source, target, sems.at[fields + i])
        for i, (source, target) in enumerate(
            ((land_sea, mask), (depth, coefs.at[0]), (east_flow, coefs.at[1]), (north_flow, coefs.at[2]))
        )
    ]
    large = [
        pltpu.make_async_copy(probes.at[c], held.at[c], sems.at[c]) for c in range(fields)
    ]
    for copy in small + large:
        copy.start()
    for copy in small:
        copy.wait()
    lane = lane_ids(rows)
    coefs[3] = mask[...].astype(jnp.float32)

    def place(index, low, high, value):
        at = HALO * index
        turned = pltpu.roll(value, at, 1) if index else value
        low = jnp.where((lane >= at) & (lane < at + HALO), turned, low)
        back = (at - HALO) % LANES
        high = jnp.where((lane >= back) & (lane < back + HALO), turned, high)
        return low, high

    def rows_out(at, value):
        low, high = value[:HALO], value[rows - HALO :]
        x_a[at] = jnp.where(even_x, high, low)
        x_b[at] = jnp.where(even_x, low, high)

    def columns_out(at, low, high):
        y_a[at] = jnp.where(even_y, high, low)
        y_b[at] = jnp.where(even_y, low, high)

    zero = jnp.zeros((rows, LANES), jnp.float32)
    low, high = zero, zero
    for a in range(4):
        value = coefs[a]
        rows_out(fields * count + a, value)
        low, high = place(a, low, high, value)
    columns_out(fields, low, high)
    for c in range(fields):
        large[c].wait()
        low, high = zero, zero
        for p in range(count):
            value = held[c, p].astype(jnp.float32) * coefs[3]
            rows_out(c * count + p, value)
            low, high = place(p, low, high, value)
        columns_out(c, low, high)


def pack(probes, depth, east_flow, north_flow, land_sea):
    fields, count, rows, cols = probes.shape
    f32 = jnp.float32
    x_shape = jax.ShapeDtypeStruct((fields * count + 4, HALO, cols), f32)
    y_shape = jax.ShapeDtypeStruct((fields + 1, rows, LANES), f32)
    return pl.pallas_call(
        pack_kernel,
        in_specs=[pl.BlockSpec(memory_space=pltpu.HBM)] * 5,
        out_shape=(
            x_shape, x_shape, y_shape, y_shape,
            jax.ShapeDtypeStruct(probes.shape, probes.dtype),
            jax.ShapeDtypeStruct((4, rows, cols), f32),
        ),
        scratch_shapes=[
            pltpu.VMEM((rows, cols), jnp.int32),
            pltpu.SemaphoreType.DMA((fields + 4,)),
        ],
        compiler_params=pltpu.CompilerParams(vmem_limit_bytes=VMEM_LIMIT),
        name="pack_edges",
    )(probes, depth, east_flow, north_flow, land_sea)


def evolve_kernel(
    probes, coefs, x_a, x_b, to_a, to_b, from_a, from_b, c_a, c_b,
    halves, gram, coef, strip_coef, strips, edges, wraps_of, state, later, flux, grid_state, total,
):
    fields, count, rows, _ = probes.shape
    own = pl.ds(TOP, rows)
    bottom = TOP + rows
    tall = rows + 2 * HALO
    first = TOP - HALO
    tiles = [(first + 8 * t, 8) for t in range(tall // 8)]
    lane8 = lane_ids(8)
    half = 0.5 * time_step
    even_x = lax.rem(lax.axis_index("gx"), 2) == 0
    even_y = lax.rem(lax.axis_index("gy"), 2) == 0

    def x_before(i):
        return jnp.where(even_x, x_b[i], x_a[i])

    def x_after(i):
        return jnp.where(even_x, x_a[i], x_b[i])

    def fold(out, at, size, values):
        deep, east, north, sea = values
        out[0, pl.ds(at, size)] = deep
        out[1, pl.ds(at, size)] = half * sea * east
        out[2, pl.ds(at, size)] = half * sea * north
        out[3, pl.ds(at, size)] = (half * gravity) * sea

    base = fields * count
    fold(coef, TOP, rows, [coefs[a] for a in range(4)])
    fold(coef, first, HALO, [x_before(base + a) for a in range(4)])
    fold(coef, bottom, HALO, [x_after(base + a) for a in range(4)])

    def kinds(k, *at):
        mine, theirs = (to_b, to_a) if k in (1, 2) else (from_b, from_a)
        if k in (2, 3):
            mine, theirs = theirs, mine
        return jnp.where(even_y, mine[at], theirs[at])

    back = (HALO, 0, HALO, 0)

    def gathered(tile_of, size, slot_of):
        lane = lane_ids(size)
        part = lax.rem(lane, 16) // HALO
        out = None
        for k in range(4):
            index = (HALO * slot_of(lane) + lax.rem(lane, HALO) - back[k] + LANES) & (LANES - 1)
            picked = jnp.take_along_axis(tile_of(k), index, axis=1)
            out = picked if out is None else jnp.where(part == k, picked, out)
        return out

    groups = count // 8

    def unpack(at, size, tile_of):
        values = [
            gathered(lambda k: tile_of(k, fields), size, lambda lane: jnp.full_like(lane, a))
            for a in range(4)
        ]
        fold(strip_coef, at, size, values)
        for c in range(fields):
            for g in range(groups):
                strips[0, c, g, pl.ds(at, size)] = gathered(
                    lambda k: tile_of(k, c), size, lambda lane: 8 * g + lane // 16
                )

    for t in range(rows // 8):
        unpack(TOP + 8 * t, 8, lambda k, c: kinds(k, c, pl.ds(8 * t, 8)))
    whole = jnp.zeros((8 - HALO, LANES), jnp.float32)
    unpack(0, 8, lambda k, c: jnp.concatenate([whole, jnp.where(even_x, c_b[k, c], c_a[k, c])], 0))
    unpack(bottom, 8, lambda k, c: jnp.concatenate([jnp.where(even_x, c_a[k, c], c_b[k, c]), whole], 0))

    def shifted(value, wrap):
        if wrap is None:
            return pltpu.roll(value, LANES - 1, 1) - pltpu.roll(value, 1, 1)
        up = jnp.where(lane8 == 0, wrap, value)
        down = jnp.where(lane8 == LANES - 1, wrap, value)
        return pltpu.roll(up, LANES - 1, 1) - pltpu.roll(down, 1, 1)

    def velocities(source, factors, wraps, write):
        for at, size in tiles:
            here, above, below = pl.ds(at, size), pl.ds(at - 1, size), pl.ds(at + 1, size)
            deep, east, north, slope = [factors[a, here] for a in range(4)]
            h, e, n = [source(c)[here] for c in range(3)]
            xh, xe, xn = [source(c)[below] - source(c)[above] for c in range(3)]
            yh, ye, yn = [shifted(v, wraps(c, here)) for c, v in enumerate((h, e, n))]
            e_new = e + (time_step * coriolis) * n - (east * xe + north * ye + slope * xh)
            n_new = n - (time_step * coriolis) * e - (east * xn + north * yn + slope * yh)
            write(at, e_new, n_new)
            flux[0, here] = deep * e_new
            flux[1, here] = deep * n_new
            flux[2, here] = h - (east * xh + north * yh)

    def heights(factors, wraps, write):
        for at, size in tiles:
            here, above, below = pl.ds(at, size), pl.ds(at - 1, size), pl.ds(at + 1, size)
            along = flux[0, below] - flux[0, above]
            across = shifted(flux[1, here], wraps(here))
            write(at, flux[2, here] - factors[3, here] * (along + across))

    def keep(slot, g, at, size, value):
        edges[slot, g, pl.ds(at, size)] = jnp.where(
            lax.rem(lane_ids(size), 16) == HALO, pltpu.roll(value, LANES - 8, 1), value
        )

    def strip_body(g, carry):
        for step in range(STEPS):
            for at, size in tiles:
                for c in range(fields):
                    keep(4 * step + c, g, at, size, strips[step, c, g, pl.ds(at, size)])

            def write_velocity(at, e_new, n_new):
                if step + 1 < STEPS:
                    strips[step + 1, 1, g, pl.ds(at, 8)] = e_new
                    strips[step + 1, 2, g, pl.ds(at, 8)] = n_new

            velocities(
                lambda c: strips.at[step, c, g], strip_coef, lambda c, here: None, write_velocity
            )
            for at, size in tiles:
                keep(4 * step + 3, g, at, size, flux[1, pl.ds(at, size)])
            if step + 1 < STEPS:

                def write_height(at, h_new):
                    strips[step + 1, 0, g, pl.ds(at, 8)] = h_new

                heights(strip_coef, lambda here: None, write_height)
        return carry

    lax.fori_loop(0, groups, strip_body, 0)

    def body(p, carry):
        group = p // 8
        turn = lax.rem(2 * LANES - 16 * lax.rem(p, 8) - HALO, LANES)
        for c in range(fields):
            state[c, own] = probes[c, p].astype(jnp.float32) * coefs[3]
            state[c, pl.ds(first, HALO)] = x_before(c * count + p)
            state[c, pl.ds(bottom, HALO)] = x_after(c * count + p)
        for slot in range(4 * STEPS):
            for at, size in tiles:
                here = pl.ds(at, size)
                wraps_of[slot, here] = pltpu.roll(edges[slot, group, here], turn, 1)

        def wrap(slot):
            return lambda here: wraps_of[slot, here]

        def row(c):
            return pl.multiple_of((c * count + p) * tall, 8)

        buffers = (state, later)
        for step in range(STEPS):
            now = buffers[step]
            last = step + 1 == STEPS

            def write_velocity(at, e_new, n_new):
                if not last:
                    later[1, pl.ds(at, 8)] = e_new
                    later[2, pl.ds(at, 8)] = n_new
                else:
                    grid_state[pl.ds(row(1) + (at - first), 8)] = e_new
                    grid_state[pl.ds(row(2) + (at - first), 8)] = n_new

            velocities(
                lambda c: now.at[c], coef, lambda c, here: wrap(4 * step + c)(here), write_velocity
            )

            def write_height(at, h_new):
                if not last:
                    later[0, pl.ds(at, 8)] = h_new
                else:
                    grid_state[pl.ds(row(0) + (at - first), 8)] = h_new

            heights(coef, wrap(4 * step + 3), write_height)
        return carry

    lax.fori_loop(0, count, body, 0)

    total[...] = jnp.zeros_like(total)

    def gram_body(i, acc):
        c, block = i // (rows // BLOCK), lax.rem(i, rows // BLOCK)
        at = c * count * tall + block * BLOCK + HALO
        values = jnp.concatenate(
            [grid_state[pl.ds(at + x, count, stride=tall)] for x in range(BLOCK)], 1
        )
        top = values.astype(jnp.bfloat16)
        low = (values - top.astype(jnp.float32)).astype(jnp.bfloat16)
        both = jnp.concatenate([top, low], 0)
        halves[i] = both
        return acc + lax.dot_general(
            both, both, (((1,), (1,)), ((), ())), preferred_element_type=jnp.float32
        )

    acc = jnp.zeros((2 * count, 2 * count), jnp.float32)
    acc = lax.fori_loop(0, fields * rows // BLOCK, gram_body, acc, unroll=4)
    total[:, : 2 * count] = acc
    value = total[...]
    summed = value[:count] + value[count:]
    summed = summed + pltpu.roll(summed, LANES - count, 1)
    lane = lane_ids(count)
    summed = jnp.where(lane < count, summed, 0.0)
    out = summed[:8]
    for b in range(1, count // 8):
        out = out + pltpu.roll(summed[8 * b : 8 * b + 8], count * b, 1)
    gram[...] = out


def evolve(probes, coefs, *received):
    fields, count, rows, cols = probes.shape
    tall = rows + 2 * TOP
    groups = count // 8
    f32 = jnp.float32
    return pl.pallas_call(
        evolve_kernel,
        out_shape=(
            jax.ShapeDtypeStruct((fields * rows // BLOCK, 2 * count, BLOCK * cols), jnp.bfloat16),
            jax.ShapeDtypeStruct((8, LANES), f32),
        ),
        scratch_shapes=[
            pltpu.VMEM((4, tall, LANES), f32),
            pltpu.VMEM((4, tall, LANES), f32),
            pltpu.VMEM((STEPS, fields, groups, tall, LANES), f32),
            pltpu.VMEM((4 * STEPS, groups, tall, LANES), f32),
            pltpu.VMEM((4 * STEPS, tall, LANES), f32),
            pltpu.VMEM((fields, tall, LANES), f32),
            pltpu.VMEM((fields, tall, LANES), f32),
            pltpu.VMEM((3, tall, LANES), f32),
            pltpu.VMEM((fields * count * (rows + 2 * HALO), LANES), f32),
            pltpu.VMEM((2 * count, LANES), f32),
        ],
        compiler_params=pltpu.CompilerParams(vmem_limit_bytes=VMEM_LIMIT),
        name="evolve_and_gram",
    )(probes, coefs, *received)


def finish_kernel(scale, grams, halves, basis, triangle, grid_out, staged, sems):
    fields, count, rows, cols = staged.shape
    stride = grid_out.shape[0] // count
    summed = jnp.sum(grams[...], 0)
    lane = lane_ids(count)
    row_id = lax.broadcasted_iota(jnp.int32, (count, LANES), 0)
    gram = jnp.concatenate(
        [summed if b == 0 else pltpu.roll(summed, LANES - count * b, 1) for b in range(count // 8)],
        0,
    )
    work = jnp.where(lane < count, gram, jnp.where(lane == row_id + count, 1.0, 0.0))
    for k in range(count):
        pivot_row = work[k : k + 1]
        ratio = work[:, k : k + 1] / work[k : k + 1, k : k + 1]
        work = work - jnp.where(row_id > k, ratio * pivot_row, 0.0)
    pivots = jnp.sum(jnp.where(lane == row_id, work, 0.0), 1, keepdims=True)
    work = work / jnp.sqrt(pivots)
    triangle[...] = jnp.where(lane >= row_id, work, 0.0)[:, :count] * (1.0 / scale)
    lower = (work * scale)[:, count : 2 * count]
    top = lower.astype(jnp.bfloat16)
    low = (lower - top.astype(jnp.float32)).astype(jnp.bfloat16)
    factor = jnp.concatenate([top, top, low], 1)

    copies = []
    for c in range(fields):

        def body(i, carry):
            both = halves[c * (rows // BLOCK) + i]
            stacked = jnp.concatenate([both, both[:count]], 0)
            out = jnp.dot(factor, stacked, preferred_element_type=jnp.float32)
            for x in range(BLOCK):
                at = BLOCK * i + x
                grid_out[pl.ds(at, count, stride=stride)] = out[:, x * cols : (x + 1) * cols]
            return carry

        lax.fori_loop(0, rows // BLOCK, body, 0, unroll=2)

        def store(q, carry):
            at = pl.multiple_of(q * stride, 8)
            staged[c, q] = grid_out[pl.ds(at, rows)].astype(jnp.bfloat16)
            return carry

        lax.fori_loop(0, count, store, 0, unroll=4)
        copies.append(pltpu.make_async_copy(staged.at[c], basis.at[c], sems.at[c]))
        copies[-1].start()
    for copy in copies:
        copy.wait()


def finish(grams, halves, shape, scale):
    fields, count, rows, cols = shape
    return pl.pallas_call(
        functools.partial(finish_kernel, scale),
        out_shape=(
            jax.ShapeDtypeStruct(shape, jnp.bfloat16),
            jax.ShapeDtypeStruct((count, count), jnp.float32),
        ),
        out_specs=(
            pl.BlockSpec(memory_space=pltpu.HBM),
            pl.BlockSpec(memory_space=pltpu.VMEM),
        ),
        scratch_shapes=[
            pltpu.VMEM((count * (rows + 8), cols), jnp.float32),
            pltpu.VMEM(shape, jnp.bfloat16),
            pltpu.SemaphoreType.DMA((fields,)),
        ],
        compiler_params=pltpu.CompilerParams(vmem_limit_bytes=VMEM_LIMIT),
        name="factor_and_apply",
    )(grams, halves)


def first_pairs(size):
    return [(i, i ^ 1) for i in range(size)]


def second_pairs(size):
    return [(i, ((i + 1) ^ 1) - 1) for i in range(1, size - 1)]


def per_device(probes, depth, east_flow, north_flow, land_sea):
    fields, count, rows, cols = probes.shape
    nx, ny = lax.axis_size("gx"), lax.axis_size("gy")
    even_x = lax.rem(lax.axis_index("gx"), 2) == 0
    x_a, x_b, to_a, to_b, held, coefs = pack(probes, depth, east_flow, north_flow, land_sea)
    from_b = lax.ppermute(to_b, "gy", second_pairs(ny))
    from_a = lax.ppermute(to_a, "gy", first_pairs(ny))
    got_xb = lax.ppermute(x_b, "gx", second_pairs(nx))
    got_xa = lax.ppermute(x_a, "gx", first_pairs(nx))
    even_y = lax.rem(lax.axis_index("gy"), 2) == 0
    rows_of = (
        jnp.where(even_y, from_b, from_a),
        jnp.where(even_y, to_b, to_a),
        jnp.where(even_y, to_a, to_b),
        jnp.where(even_y, from_a, from_b),
    )
    low = jnp.stack([k[:, :HALO] for k in rows_of])
    high = jnp.stack([k[:, rows - HALO :] for k in rows_of])
    c_b = lax.ppermute(jnp.where(even_x, low, high), "gx", second_pairs(nx))
    c_a = lax.ppermute(jnp.where(even_x, high, low), "gx", first_pairs(nx))
    halves, gram = evolve(held, coefs, got_xa, got_xb, to_a, to_b, from_a, from_b, c_a, c_b)
    devices = nx * ny
    grams = lax.all_to_all(
        jnp.broadcast_to(gram[None], (devices,) + gram.shape), ("gx", "gy"), 0, 0
    )
    scale = math.sqrt(fields * rows * nx * cols * ny)
    return finish(grams, halves, probes.shape, scale)


def solution(mesh):
    in_specs = (
        P(None, None, "gx", "gy"),
        P("gx", "gy"),
        P("gx", "gy"),
        P("gx", "gy"),
        P("gx", "gy"),
    )
    out_specs = (P(None, None, "gx", "gy"), P())
    return jax.shard_map(
        per_device, mesh=mesh, in_specs=in_specs, out_specs=out_specs, check_vma=False
    )
```

```python
import functools
import math

import jax
import jax.numpy as jnp
from jax import lax
from jax.experimental import pallas as pl
from jax.experimental.pallas import tpu as pltpu
from jax.sharding import PartitionSpec as P

STEPS = 2
HALO = 2 * STEPS
LANES = 128
TOP = 8

time_step = 0.3
coriolis = 0.5
gravity = 1.0

VMEM_LIMIT = 24 * 1024 * 1024
BLOCK = 8
JOIN = 1
WIDE = 4


def lane_ids(rows):
    return lax.broadcasted_iota(jnp.int32, (rows, LANES), 1)


def pack_kernel(
    probes, depth, east_flow, north_flow, land_sea,
    x_a, x_b, y_a, y_b, held, coefs, mask, sems,
):
    fields, count, rows, _ = held.shape
    even_x = lax.rem(lax.axis_index("gx"), 2) == 0
    even_y = lax.rem(lax.axis_index("gy"), 2) == 0
    small = [
        pltpu.make_async_copy(source, target, sems.at[fields + i])
        for i, (source, target) in enumerate(
            ((land_sea, mask), (depth, coefs.at[0]), (east_flow, coefs.at[1]), (north_flow, coefs.at[2]))
        )
    ]
    large = [
        pltpu.make_async_copy(probes.at[c], held.at[c], sems.at[c]) for c in range(fields)
    ]
    for copy in small + large:
        copy.start()
    for copy in small:
        copy.wait()
    lane = lane_ids(rows)
    coefs[3] = mask[...].astype(jnp.float32)

    def place(index, low, high, value):
        at = HALO * index
        turned = pltpu.roll(value, at, 1) if index else value
        low = jnp.where((lane >= at) & (lane < at + HALO), turned, low)
        back = (at - HALO) % LANES
        high = jnp.where((lane >= back) & (lane < back + HALO), turned, high)
        return low, high

    def rows_out(at, value):
        low, high = value[:HALO], value[rows - HALO :]
        x_a[at] = jnp.where(even_x, high, low)
        x_b[at] = jnp.where(even_x, low, high)

    def columns_out(at, low, high):
        y_a[at] = jnp.where(even_y, high, low)
        y_b[at] = jnp.where(even_y, low, high)

    zero = jnp.zeros((rows, LANES), jnp.float32)
    low, high = zero, zero
    for a in range(4):
        value = coefs[a]
        rows_out(fields * count + a, value)
        low, high = place(a, low, high, value)
    columns_out(fields, low, high)
    for c in range(fields):
        large[c].wait()
        low, high = zero, zero
        for p in range(count):
            value = held[c, p].astype(jnp.float32) * coefs[3]
            rows_out(c * count + p, value)
            low, high = place(p, low, high, value)
        columns_out(c, low, high)


def pack(*arguments):
    probes = arguments[0]
    fields, count, rows, cols = probes.shape
    f32 = jnp.float32
    x_shape = jax.ShapeDtypeStruct((fields * count + 4, HALO, cols), f32)
    y_shape = jax.ShapeDtypeStruct((fields + 1, rows, LANES), f32)
    return pl.pallas_call(
        pack_kernel,
        in_specs=[pl.BlockSpec(memory_space=pltpu.HBM)] * 5,
        out_shape=(
            x_shape, x_shape, y_shape, y_shape,
            jax.ShapeDtypeStruct(probes.shape, probes.dtype),
            jax.ShapeDtypeStruct((4, rows, cols), f32),
        ),
        scratch_shapes=[
            pltpu.VMEM((rows, cols), jnp.int32),
            pltpu.SemaphoreType.DMA((fields + 4,)),
        ],
        compiler_params=pltpu.CompilerParams(vmem_limit_bytes=VMEM_LIMIT),
        name="pack_edges",
    )(*[pltpu.with_memory_space_constraint(v, pltpu.HBM) for v in arguments])


def evolve_kernel(
    probes, coefs, x_a, x_b, to_a, to_b, from_a, from_b, c_a, c_b,
    halves, gram, coef, strip_coef, strips, edges, weights,
    wraps_of, state, later, flux, slope, grid_state, total,
):
    fields, count, rows, _ = probes.shape
    own = pl.ds(TOP, rows)
    bottom = TOP + rows
    tall = rows + 2 * HALO
    first = TOP - HALO
    tiles = [(first + 8 * t, 8) for t in range(tall // 8)]
    padded = 16 * ((tall + 15) // 16)
    window = pl.ds(first, padded)
    lane8 = lane_ids(8)
    half = 0.5 * time_step
    even_x = lax.rem(lax.axis_index("gx"), 2) == 0
    even_y = lax.rem(lax.axis_index("gy"), 2) == 0

    def x_before(i):
        return jnp.where(even_x, x_b[i], x_a[i])

    def x_after(i):
        return jnp.where(even_x, x_a[i], x_b[i])

    def fold(out, at, size, values):
        deep, east, north, sea = values
        out[0, pl.ds(at, size)] = deep
        out[1, pl.ds(at, size)] = half * sea * east
        out[2, pl.ds(at, size)] = half * sea * north
        out[3, pl.ds(at, size)] = (half * gravity) * sea

    base = fields * count
    fold(coef, TOP, rows, [coefs[a] for a in range(4)])
    fold(coef, first, HALO, [x_before(base + a) for a in range(4)])
    fold(coef, bottom, HALO, [x_after(base + a) for a in range(4)])

    def kinds(k, *at):
        mine, theirs = (to_b, to_a) if k in (1, 2) else (from_b, from_a)
        if k in (2, 3):
            mine, theirs = theirs, mine
        return jnp.where(even_y, mine[at], theirs[at])

    back = (HALO, 0, HALO, 0)

    def gathered(tile_of, size, slot_of):
        lane = lane_ids(size)
        part = lax.rem(lane, 16) // HALO
        out = None
        for k in range(4):
            index = (HALO * slot_of(lane) + lax.rem(lane, HALO) - back[k] + LANES) & (LANES - 1)
            picked = jnp.take_along_axis(tile_of(k), index, axis=1)
            out = picked if out is None else jnp.where(part == k, picked, out)
        return out

    groups = count // 8

    def unpack(at, size, tile_of):
        values = [
            gathered(lambda k: tile_of(k, fields), size, lambda lane: jnp.full_like(lane, a))
            for a in range(4)
        ]
        fold(strip_coef, at, size, values)
        for c in range(fields):
            for g in range(groups):
                strips[0, c, g, pl.ds(at, size)] = gathered(
                    lambda k: tile_of(k, c), size, lambda lane: 8 * g + lane // 16
                )

    for t in range(rows // 8):
        unpack(TOP + 8 * t, 8, lambda k, c: kinds(k, c, pl.ds(8 * t, 8)))
    whole = jnp.zeros((8 - HALO, LANES), jnp.float32)
    unpack(0, 8, lambda k, c: jnp.concatenate([whole, jnp.where(even_x, c_b[k, c], c_a[k, c])], 0))
    unpack(bottom, 8, lambda k, c: jnp.concatenate([jnp.where(even_x, c_a[k, c], c_b[k, c]), whole], 0))

    source = lax.broadcasted_iota(jnp.int32, (2 * LANES, LANES), 0) & (LANES - 1)
    target = lax.broadcasted_iota(jnp.int32, (2 * LANES, LANES), 1)
    weights[...] = (
        (source == target + 1).astype(jnp.float32) - (source == target - 1).astype(jnp.float32)
    ).astype(jnp.bfloat16)

    def two(value):
        top = value.astype(jnp.bfloat16)
        return top, (value - top.astype(jnp.float32)).astype(jnp.bfloat16)

    def shifted(value, wrap):
        if wrap is None:
            return pltpu.roll(value, LANES - 1, 1) - pltpu.roll(value, 1, 1)
        up = jnp.where(lane8 == 0, wrap, value)
        down = jnp.where(lane8 == LANES - 1, wrap, value)
        return pltpu.roll(up, LANES - 1, 1) - pltpu.roll(down, 1, 1)

    def velocities(source, factors, differences, flux, write):
        for at, size in tiles:
            here, above, below = pl.ds(at, size), pl.ds(at - 1, size), pl.ds(at + 1, size)
            deep, east, north, slope = [factors[a, here] for a in range(4)]
            h, e, n = [source(c)[here] for c in range(3)]
            xh, xe, xn = [source(c)[below] - source(c)[above] for c in range(3)]
            yh, ye, yn = [differences(c, at, v) for c, v in enumerate((h, e, n))]
            e_new = e + (time_step * coriolis) * n - (east * xe + north * ye + slope * xh)
            n_new = n - (time_step * coriolis) * e - (east * xn + north * yn + slope * yh)
            write(at, e_new, n_new)
            flux[0, here] = deep * e_new
            flux[1, here] = deep * n_new
            flux[2, here] = h - (east * xh + north * yh)

    def heights(factors, differences, flux, write):
        for at, size in tiles:
            here, above, below = pl.ds(at, size), pl.ds(at - 1, size), pl.ds(at + 1, size)
            along = flux[0, below] - flux[0, above]
            across = differences(at)
            write(at, flux[2, here] - factors[3, here] * (along + across))

    def keep(slot, g, at, size, value):
        edges[slot, g, pl.ds(at, size)] = jnp.where(
            lax.rem(lane_ids(size), 16) == HALO, pltpu.roll(value, LANES - 8, 1), value
        )

    def strip_body(g, carry):
        mine = flux.at[0]
        for step in range(STEPS):
            for at, size in tiles:
                for c in range(fields):
                    keep(4 * step + c, g, at, size, strips[step, c, g, pl.ds(at, size)])

            def write_velocity(at, e_new, n_new):
                if step + 1 < STEPS:
                    strips[step + 1, 1, g, pl.ds(at, 8)] = e_new
                    strips[step + 1, 2, g, pl.ds(at, 8)] = n_new

            velocities(
                lambda c: strips.at[step, c, g], strip_coef,
                lambda c, at, value: shifted(value, None), mine, write_velocity,
            )
            for at, size in tiles:
                value = mine[1, pl.ds(at, size)]
                part = lax.rem(lane8, 16)
                edges[4 * step + 3, g, pl.ds(at, size)] = jnp.where(
                    part == HALO, -pltpu.roll(value, 1, 1), pltpu.roll(value, LANES - 9, 1)
                )
            if step + 1 < STEPS:

                def write_height(at, h_new):
                    strips[step + 1, 0, g, pl.ds(at, 8)] = h_new

                heights(
                    strip_coef, lambda at: shifted(mine[1, pl.ds(at, 8)], None), mine, write_height
                )
        return carry

    lax.fori_loop(0, groups, strip_body, 0)

    ends = (lane8 == 0) | (lane8 == LANES - 1)

    def body(i, carry):
        def begin(k):
            p = WIDE * i + k
            group, slot = p // 8, lax.rem(p, 8)
            turn = lax.rem(2 * LANES - 16 * slot - HALO, LANES)
            for c in range(fields):
                state[k, c, own] = probes[c, p].astype(jnp.float32) * coefs[3]
                state[k, c, pl.ds(first, HALO)] = x_before(c * count + p)
                state[k, c, pl.ds(bottom, HALO)] = x_after(c * count + p)
            for slot in range(4 * STEPS):
                for at, size in tiles:
                    here = pl.ds(at, size)
                    wraps_of[k, slot, here] = pltpu.roll(edges[slot, group, here], turn, 1)

        for k in range(WIDE):
            begin(k)

        for step in range(STEPS):
            last = step + 1 == STEPS
            for k in range(WIDE):

                def row(c):
                    return pl.multiple_of((c * count + WIDE * i + k) * tall, 8)

                def write_velocity(at, e_new, n_new):
                    if not last:
                        later[k, 1, pl.ds(at, 8)] = e_new
                        later[k, 2, pl.ds(at, 8)] = n_new
                    else:
                        grid_state[pl.ds(row(1) + (at - first), 8)] = e_new
                        grid_state[pl.ds(row(2) + (at - first), 8)] = n_new

                now = (state, later)[step]
                velocities(
                    lambda c: now.at[k, c], coef,
                    lambda c, at, value: shifted(value, wraps_of[k, 4 * step + c, pl.ds(at, 8)]),
                    flux.at[k], write_velocity,
                )
            for j in range(0, WIDE, JOIN):
                left = jnp.concatenate(
                    [jnp.concatenate(two(flux[k, 1, window]), 1) for k in range(j, j + JOIN)], 0
                )
                slope[j * padded : (j + JOIN) * padded] = jnp.dot(
                    left, weights[...], preferred_element_type=jnp.float32
                )
            for k in range(WIDE):

                def row(c):
                    return pl.multiple_of((c * count + WIDE * i + k) * tall, 8)

                def write_height(at, h_new):
                    if not last:
                        later[k, 0, pl.ds(at, 8)] = h_new
                    else:
                        grid_state[pl.ds(row(0) + (at - first), 8)] = h_new

                def across(at):
                    wrap = wraps_of[k, 4 * step + 3, pl.ds(at, 8)]
                    return slope[pl.ds(k * padded + at - first, 8)] + jnp.where(ends, wrap, 0.0)

                heights(coef, across, flux.at[k], write_height)
        return carry

    lax.fori_loop(0, count // WIDE, body, 0)

    total[...] = jnp.zeros_like(total)

    def gram_body(i, acc):
        c, block = i // (rows // BLOCK), lax.rem(i, rows // BLOCK)
        at = c * count * tall + block * BLOCK + HALO
        values = jnp.concatenate(
            [grid_state[pl.ds(at + x, count, stride=tall)] for x in range(BLOCK)], 1
        )
        top = values.astype(jnp.bfloat16)
        low = (values - top.astype(jnp.float32)).astype(jnp.bfloat16)
        both = jnp.concatenate([top, low], 0)
        halves[i] = both
        return acc + lax.dot_general(
            both, both, (((1,), (1,)), ((), ())), preferred_element_type=jnp.float32
        )

    acc = jnp.zeros((2 * count, 2 * count), jnp.float32)
    acc = lax.fori_loop(0, fields * rows // BLOCK, gram_body, acc, unroll=4)
    total[:, : 2 * count] = acc
    value = total[...]
    summed = value[:count] + value[count:]
    summed = summed + pltpu.roll(summed, LANES - count, 1)
    lane = lane_ids(count)
    summed = jnp.where(lane < count, summed, 0.0)
    out = summed[:8]
    for b in range(1, count // 8):
        out = out + pltpu.roll(summed[8 * b : 8 * b + 8], count * b, 1)
    gram[...] = out


def evolve(probes, coefs, *received):
    fields, count, rows, cols = probes.shape
    padded = 16 * ((rows + 2 * HALO + 15) // 16)
    tall = padded + TOP
    groups = count // 8
    f32 = jnp.float32
    return pl.pallas_call(
        evolve_kernel,
        out_shape=(
            jax.ShapeDtypeStruct((fields * rows // BLOCK, 2 * count, BLOCK * cols), jnp.bfloat16),
            jax.ShapeDtypeStruct((8, LANES), f32),
        ),
        scratch_shapes=[
            pltpu.VMEM((4, tall, LANES), f32),
            pltpu.VMEM((4, tall, LANES), f32),
            pltpu.VMEM((STEPS, fields, groups, tall, LANES), f32),
            pltpu.VMEM((4 * STEPS, groups, tall, LANES), f32),
            pltpu.VMEM((2 * LANES, LANES), jnp.bfloat16),
            pltpu.VMEM((WIDE, 4 * STEPS, tall, LANES), f32),
            pltpu.VMEM((WIDE, fields, tall, LANES), f32),
            pltpu.VMEM((WIDE, fields, tall, LANES), f32),
            pltpu.VMEM((WIDE, 3, tall, LANES), f32),
            pltpu.VMEM((WIDE * padded, LANES), f32),
            pltpu.VMEM((fields * count * (rows + 2 * HALO), LANES), f32),
            pltpu.VMEM((2 * count, LANES), f32),
        ],
        compiler_params=pltpu.CompilerParams(vmem_limit_bytes=VMEM_LIMIT),
        name="evolve_and_gram",
    )(probes, coefs, *received)


def finish_kernel(scale, grams, halves, basis, triangle, grid_out, staged, sems):
    fields, count, rows, cols = staged.shape
    stride = grid_out.shape[0] // count
    summed = jnp.sum(grams[...], 0)
    lane = lane_ids(count)
    row_id = lax.broadcasted_iota(jnp.int32, (count, LANES), 0)
    gram = jnp.concatenate(
        [summed if b == 0 else pltpu.roll(summed, LANES - count * b, 1) for b in range(count // 8)],
        0,
    )
    work = jnp.where(lane < count, gram, jnp.where(lane == row_id + count, 1.0, 0.0))
    for k in range(count):
        pivot_row = work[k : k + 1]
        ratio = work[:, k : k + 1] / work[k : k + 1, k : k + 1]
        work = work - jnp.where(row_id > k, ratio * pivot_row, 0.0)
    pivots = jnp.sum(jnp.where(lane == row_id, work, 0.0), 1, keepdims=True)
    work = work / jnp.sqrt(pivots)
    triangle[...] = jnp.where(lane >= row_id, work, 0.0)[:, :count] * (1.0 / scale)
    lower = (work * scale)[:, count : 2 * count]
    top = lower.astype(jnp.bfloat16)
    low = (lower - top.astype(jnp.float32)).astype(jnp.bfloat16)
    factor = jnp.concatenate([top, top, low], 1)

    copies = []
    for c in range(fields):

        def body(i, carry):
            both = halves[c * (rows // BLOCK) + i]
            stacked = jnp.concatenate([both, both[:count]], 0)
            out = jnp.dot(factor, stacked, preferred_element_type=jnp.float32)
            for x in range(BLOCK):
                at = BLOCK * i + x
                grid_out[pl.ds(at, count, stride=stride)] = out[:, x * cols : (x + 1) * cols]
            return carry

        lax.fori_loop(0, rows // BLOCK, body, 0, unroll=2)

        def store(q, carry):
            at = pl.multiple_of(q * stride, 8)
            staged[c, q] = grid_out[pl.ds(at, rows)].astype(jnp.bfloat16)
            return carry

        lax.fori_loop(0, count, store, 0, unroll=4)
        copies.append(pltpu.make_async_copy(staged.at[c], basis.at[c], sems.at[c]))
        copies[-1].start()
    for copy in copies:
        copy.wait()


def finish(grams, halves, shape, scale):
    fields, count, rows, cols = shape
    return pl.pallas_call(
        functools.partial(finish_kernel, scale),
        out_shape=(
            jax.ShapeDtypeStruct(shape, jnp.bfloat16),
            jax.ShapeDtypeStruct((count, count), jnp.float32),
        ),
        out_specs=(
            pl.BlockSpec(memory_space=pltpu.HBM),
            pl.BlockSpec(memory_space=pltpu.VMEM),
        ),
        scratch_shapes=[
            pltpu.VMEM((count * (rows + 8), cols), jnp.float32),
            pltpu.VMEM(shape, jnp.bfloat16),
            pltpu.SemaphoreType.DMA((fields,)),
        ],
        compiler_params=pltpu.CompilerParams(vmem_limit_bytes=VMEM_LIMIT),
        name="factor_and_apply",
    )(grams, halves)


def first_pairs(size):
    return [(i, i ^ 1) for i in range(size)]


def second_pairs(size):
    return [(i, ((i + 1) ^ 1) - 1) for i in range(1, size - 1)]


def per_device(probes, depth, east_flow, north_flow, land_sea):
    fields, count, rows, cols = probes.shape
    nx, ny = lax.axis_size("gx"), lax.axis_size("gy")
    even_x = lax.rem(lax.axis_index("gx"), 2) == 0
    x_a, x_b, to_a, to_b, held, coefs = pack(probes, depth, east_flow, north_flow, land_sea)
    from_b = lax.ppermute(to_b, "gy", second_pairs(ny))
    from_a = lax.ppermute(to_a, "gy", first_pairs(ny))
    got_xb = lax.ppermute(x_b, "gx", second_pairs(nx))
    got_xa = lax.ppermute(x_a, "gx", first_pairs(nx))
    even_y = lax.rem(lax.axis_index("gy"), 2) == 0
    rows_of = (
        jnp.where(even_y, from_b, from_a),
        jnp.where(even_y, to_b, to_a),
        jnp.where(even_y, to_a, to_b),
        jnp.where(even_y, from_a, from_b),
    )
    low = jnp.stack([k[:, :HALO] for k in rows_of])
    high = jnp.stack([k[:, rows - HALO :] for k in rows_of])
    c_b = lax.ppermute(jnp.where(even_x, low, high), "gx", second_pairs(nx))
    c_a = lax.ppermute(jnp.where(even_x, high, low), "gx", first_pairs(nx))
    halves, gram = evolve(held, coefs, got_xa, got_xb, to_a, to_b, from_a, from_b, c_a, c_b)
    devices = nx * ny
    grams = lax.all_to_all(
        jnp.broadcast_to(gram[None], (devices,) + gram.shape), ("gx", "gy"), 0, 0
    )
    scale = math.sqrt(fields * rows * nx * cols * ny)
    return finish(grams, halves, probes.shape, scale)


def solution(mesh):
    in_specs = (
        P(None, None, "gx", "gy"),
        P("gx", "gy"),
        P("gx", "gy"),
        P("gx", "gy"),
        P("gx", "gy"),
    )
    out_specs = (P(None, None, "gx", "gy"), P())
    return jax.shard_map(
        per_device, mesh=mesh, in_specs=in_specs, out_specs=out_specs, check_vma=False
    )
```

```python
import functools
import math

import jax
import jax.numpy as jnp
from jax import lax
from jax.experimental import pallas as pl
from jax.experimental.pallas import tpu as pltpu
from jax.sharding import PartitionSpec as P

STEPS = 2
HALO = 2 * STEPS
LANES = 128
TOP = 8

time_step = 0.3
coriolis = 0.5
gravity = 1.0

MIB = 1024 * 1024
BLOCK = 8
PARTS = 2
PIVOTS = 8
WIDE = 8


def lane_ids(rows):
    return lax.broadcasted_iota(jnp.int32, (rows, LANES), 1)


def in_hbm(arrays):
    return [pltpu.with_memory_space_constraint(v, pltpu.HBM) for v in arrays]


def pack_kernel(
    probes, depth, east_flow, north_flow, land_sea,
    x_a, x_b, y_a, y_b, held, coefs, mask, sems,
):
    fields, count, rows, _ = held.shape
    even_x = lax.rem(lax.axis_index("gx"), 2) == 0
    even_y = lax.rem(lax.axis_index("gy"), 2) == 0
    small = [
        pltpu.make_async_copy(source, target, sems.at[fields + i])
        for i, (source, target) in enumerate(
            ((land_sea, mask), (depth, coefs.at[0]), (east_flow, coefs.at[1]), (north_flow, coefs.at[2]))
        )
    ]
    large = [
        pltpu.make_async_copy(probes.at[c], held.at[c], sems.at[c]) for c in range(fields)
    ]
    for copy in small + large:
        copy.start()
    for copy in small:
        copy.wait()
    lane = lane_ids(rows)
    coefs[3] = mask[...].astype(jnp.float32)

    def place(index, low, high, value):
        at = HALO * index
        turned = pltpu.roll(value, at, 1) if index else value
        low = jnp.where((lane >= at) & (lane < at + HALO), turned, low)
        back = (at - HALO) % LANES
        high = jnp.where((lane >= back) & (lane < back + HALO), turned, high)
        return low, high

    def rows_out(at, value):
        low, high = value[:HALO], value[rows - HALO :]
        x_a[at] = jnp.where(even_x, high, low)
        x_b[at] = jnp.where(even_x, low, high)

    def columns_out(at, low, high):
        y_a[at] = jnp.where(even_y, high, low)
        y_b[at] = jnp.where(even_y, low, high)

    zero = jnp.zeros((rows, LANES), jnp.float32)
    low, high = zero, zero
    for a in range(4):
        value = coefs[a]
        rows_out(fields * count + a, value)
        low, high = place(a, low, high, value)
    columns_out(fields, low, high)
    for c in range(fields):
        large[c].wait()
        low, high = zero, zero
        for p in range(count):
            value = held[c, p].astype(jnp.float32) * coefs[3]
            rows_out(c * count + p, value)
            low, high = place(p, low, high, value)
        columns_out(c, low, high)


def pack(*arguments):
    probes = arguments[0]
    fields, count, rows, cols = probes.shape
    f32 = jnp.float32
    x_shape = jax.ShapeDtypeStruct((fields * count + 4, HALO, cols), f32)
    y_shape = jax.ShapeDtypeStruct((fields + 1, rows, LANES), f32)
    return pl.pallas_call(
        pack_kernel,
        in_specs=[pl.BlockSpec(memory_space=pltpu.HBM)] * 5,
        out_shape=(
            x_shape, x_shape, y_shape, y_shape,
            jax.ShapeDtypeStruct(probes.shape, probes.dtype),
        ),
        scratch_shapes=[
            pltpu.VMEM((4, rows, cols), f32),
            pltpu.VMEM((rows, cols), jnp.int32),
            pltpu.SemaphoreType.DMA((fields + 4,)),
        ],
        compiler_params=pltpu.CompilerParams(vmem_limit_bytes=16 * MIB),
        name="pack_edges",
    )(*in_hbm(arguments))


class Grid:
    def __init__(self, rows):
        self.rows = rows
        self.own = pl.ds(TOP, rows)
        self.bottom = TOP + rows
        self.first = TOP - HALO
        self.tall = rows + 2 * HALO
        self.tiles = [self.first + 8 * t for t in range(self.tall // 8)]
        self.padded = 16 * ((self.tall + 15) // 16)
        self.window = pl.ds(self.first, self.padded)
        self.height = self.padded + TOP
        self.middle = self.tiles[1:-1]
        self.outer = [self.tiles[0], self.tiles[-1]]
        self.around = [self.tiles[0], self.tiles[1], self.tiles[-2], self.tiles[-1]]


def fold(out, at, size, values):
    deep, east, north, sea = values
    half = 0.5 * time_step
    out[0, pl.ds(at, size)] = deep
    out[1, pl.ds(at, size)] = half * sea * east
    out[2, pl.ds(at, size)] = half * sea * north
    out[3, pl.ds(at, size)] = (half * gravity) * sea


def unpack(at, size, tile_of, strip_coef, strips, fields, groups):
    back = (HALO, 0, HALO, 0)
    lane = lane_ids(size)
    part = lax.rem(lane, 16) // HALO

    def gathered(plane, slot):
        out = None
        for k in range(4):
            index = (HALO * slot + lax.rem(lane, HALO) - back[k] + LANES) & (LANES - 1)
            picked = jnp.take_along_axis(tile_of(k, plane), index, axis=1)
            out = picked if out is None else jnp.where(part == k, picked, out)
        return out

    fold(strip_coef, at, size, [gathered(fields, jnp.full_like(lane, a)) for a in range(4)])
    for c in range(fields):
        for g in range(groups):
            strips[c, g, pl.ds(at, size)] = gathered(c, 8 * g + lane // 16)


def two(value):
    top = value.astype(jnp.bfloat16)
    return top, (value - top.astype(jnp.float32)).astype(jnp.bfloat16)


def shifted(value, wrap):
    lane = lane_ids(8)
    up = value if wrap is None else jnp.where(lane == 0, wrap, value)
    down = value if wrap is None else jnp.where(lane == LANES - 1, wrap, value)
    return pltpu.roll(up, LANES - 1, 1) - pltpu.roll(down, 1, 1)


def ends():
    lane = lane_ids(8)
    return (lane == 0) | (lane == LANES - 1)


def velocities(tiles, source, factors, differences, flux, write):
    for at in tiles:
        here, above, below = pl.ds(at, 8), pl.ds(at - 1, 8), pl.ds(at + 1, 8)
        deep, east, north, slope = [factors[a, here] for a in range(4)]
        h, e, n = [source(c)[here] for c in range(3)]
        xh, xe, xn = [source(c)[below] - source(c)[above] for c in range(3)]
        yh, ye, yn = [differences(c, at, v) for c, v in enumerate((h, e, n))]
        e_new = e + (time_step * coriolis) * n - (east * xe + north * ye + slope * xh)
        n_new = n - (time_step * coriolis) * e - (east * xn + north * yn + slope * yh)
        write(at, e_new, n_new)
        flux[0, here] = deep * e_new
        flux[1, here] = deep * n_new
        flux[2, here] = h - (east * xh + north * yh)


def heights(tiles, factors, across, flux, write):
    for at in tiles:
        here, above, below = pl.ds(at, 8), pl.ds(at - 1, 8), pl.ds(at + 1, 8)
        along = flux[0, below] - flux[0, above]
        write(at, flux[2, here] - factors[3, here] * (along + across(at)))


def plain(c, at, value):
    return shifted(value, None)


def keep(edges, slot, g, at, value):
    here = lax.rem(lane_ids(8), 16) == HALO
    edges[slot, g, pl.ds(at, 8)] = jnp.where(here, pltpu.roll(value, LANES - 8, 1), value)


def keep_flux(edges, slot, g, at, value):
    here = lax.rem(lane_ids(8), 16) == HALO
    edges[slot, g, pl.ds(at, 8)] = jnp.where(
        here, -pltpu.roll(value, 1, 1), pltpu.roll(value, LANES - 9, 1)
    )


def strip_velocities(tiles, written, g, now, later, strip_coef, flux, edges, slot):
    for at in tiles:
        for c in range(3):
            keep(edges, slot + c, g, at, now[c, g, pl.ds(at, 8)])

    def write(at, e_new, n_new):
        if later is not None and at in written:
            later[1, g, pl.ds(at, 8)] = e_new
            later[2, g, pl.ds(at, 8)] = n_new

    velocities(tiles, lambda c: now.at[c, g], strip_coef, plain, flux, write)
    for at in tiles:
        keep_flux(edges, slot + 3, g, at, flux[1, pl.ds(at, 8)])


def strip_heights(tiles, g, later, strip_coef, flux):
    def write(at, h_new):
        later[0, g, pl.ds(at, 8)] = h_new

    heights(tiles, strip_coef, lambda at: shifted(flux[1, pl.ds(at, 8)], None), flux, write)


def difference_weights():
    source = lax.broadcasted_iota(jnp.int32, (2 * LANES, LANES), 0) & (LANES - 1)
    target = lax.broadcasted_iota(jnp.int32, (2 * LANES, LANES), 1)
    plus = (source == target + 1).astype(jnp.float32)
    minus = (source == target - 1).astype(jnp.float32)
    return (plus - minus).astype(jnp.bfloat16)


def flux_products(grid, flux, slope, weights):
    for k in range(WIDE):
        slope[k * grid.padded : (k + 1) * grid.padded] = jnp.dot(
            jnp.concatenate(two(flux[k, 1, grid.window]), 1),
            weights[...],
            preferred_element_type=jnp.float32,
        )


def turn_of(p):
    return lax.rem(2 * LANES - 16 * lax.rem(p, 8) - HALO, LANES)


def middle_kernel(
    probes, depth, east_flow, north_flow, land_sea, to_a, to_b, from_a, from_b,
    inner, coef, strip_coef, start, after_one,
    raw, mask, edges, weights, wraps_of, state, flux, slope, sems,
):
    fields, count, rows, _ = probes.shape
    grid = Grid(rows)
    groups = count // 8
    copies = [
        pltpu.make_async_copy(source, target, sems.at[i])
        for i, (source, target) in enumerate(
            ((land_sea, mask), (depth, raw.at[0]), (east_flow, raw.at[1]), (north_flow, raw.at[2]))
        )
    ]
    for copy in copies:
        copy.start()
    weights[...] = difference_weights()
    even_y = lax.rem(lax.axis_index("gy"), 2) == 0

    def kinds(k, *at):
        mine, theirs = (to_b, to_a) if k in (1, 2) else (from_b, from_a)
        if k in (2, 3):
            mine, theirs = theirs, mine
        return jnp.where(even_y, mine[at], theirs[at])

    for t in range(rows // 8):
        unpack(
            TOP + 8 * t, 8, lambda k, c: kinds(k, c, pl.ds(8 * t, 8)), strip_coef, start, fields, groups
        )

    def strip_body(g, carry):
        strip_velocities(
            grid.tiles, grid.middle, g, start, after_one, strip_coef, flux.at[0], edges, 0
        )
        strip_heights(grid.middle, g, after_one, strip_coef, flux.at[0])
        return carry

    lax.fori_loop(0, groups, strip_body, 0)
    for copy in copies:
        copy.wait()
    raw[3] = mask[...].astype(jnp.float32)
    fold(coef, TOP, rows, [raw[a] for a in range(4)])

    def body(i, carry):
        for k in range(WIDE):
            p = WIDE * i + k
            for c in range(fields):
                state[k, c, grid.own] = probes[c, p].astype(jnp.float32) * raw[3]
            for slot in range(4):
                for at in grid.tiles:
                    here = pl.ds(at, 8)
                    wraps_of[k, slot, here] = pltpu.roll(edges[slot, p // 8, here], turn_of(p), 1)
        for k in range(WIDE):
            p = WIDE * i + k

            def write_velocity(at, e_new, n_new):
                if at in grid.middle:
                    inner[p, 1, pl.ds(at - grid.middle[0], 8)] = e_new
                    inner[p, 2, pl.ds(at - grid.middle[0], 8)] = n_new

            velocities(
                grid.tiles, lambda c: state.at[k, c], coef,
                lambda c, at, value: shifted(value, wraps_of[k, c, pl.ds(at, 8)]),
                flux.at[k], write_velocity,
            )
        flux_products(grid, flux, slope, weights)
        for k in range(WIDE):
            p = WIDE * i + k

            def write_height(at, h_new):
                inner[p, 0, pl.ds(at - grid.middle[0], 8)] = h_new

            def across(at):
                wrap = wraps_of[k, 3, pl.ds(at, 8)]
                known = slope[pl.ds(k * grid.padded + at - grid.first, 8)]
                return known + jnp.where(ends(), wrap, 0.0)

            heights(grid.middle, coef, across, flux.at[k], write_height)
        return carry

    lax.fori_loop(0, count // WIDE, body, 0)


def middle(probes, arguments, *edges):
    fields, count, rows, cols = probes.shape
    grid = Grid(rows)
    f32, groups, height = jnp.float32, count // 8, grid.height
    full = jax.ShapeDtypeStruct((fields, groups, height, LANES), f32)
    factors = jax.ShapeDtypeStruct((4, height, LANES), f32)
    vmem, hbm = pl.BlockSpec(memory_space=pltpu.VMEM), pl.BlockSpec(memory_space=pltpu.HBM)
    return pl.pallas_call(
        middle_kernel,
        in_specs=[vmem] + [hbm] * 4 + [vmem] * 4,
        out_shape=(
            jax.ShapeDtypeStruct((count, fields, 8 * len(grid.middle), LANES), f32),
            factors, factors, full, full,
        ),
        scratch_shapes=[
            pltpu.VMEM((4, rows, cols), f32),
            pltpu.VMEM((rows, cols), jnp.int32),
            pltpu.VMEM((4, groups, height, LANES), f32),
            pltpu.VMEM((2 * LANES, LANES), jnp.bfloat16),
            pltpu.VMEM((WIDE, 4, height, LANES), f32),
            pltpu.VMEM((WIDE, fields, height, LANES), f32),
            pltpu.VMEM((WIDE, 3, height, LANES), f32),
            pltpu.VMEM((WIDE * grid.padded, LANES), f32),
            pltpu.SemaphoreType.DMA((4,)),
        ],
        compiler_params=pltpu.CompilerParams(vmem_limit_bytes=24 * MIB),
        cost_estimate=pl.CostEstimate(flops=10**8, bytes_accessed=10**7, transcendentals=0),
        name="first_step",
    )(probes, *in_hbm(arguments), *edges)


def evolve_kernel(
    probes, inner, coef_in, strip_coef_in, start_in, after_one_in, x_a, x_b, c_a, c_b,
    halves, gram, coef, strip_coef, start, after_one, edges, weights,
    wraps_of, state, later, flux, slope, grid_state, total,
):
    fields, count, rows, _ = probes.shape
    grid = Grid(rows)
    groups = count // 8
    tall, first, bottom = grid.tall, grid.first, grid.bottom
    even_x = lax.rem(lax.axis_index("gx"), 2) == 0
    weights[...] = difference_weights()

    def x_before(i):
        return jnp.where(even_x, x_b[i], x_a[i])

    def x_after(i):
        return jnp.where(even_x, x_a[i], x_b[i])

    base = fields * count
    coef[:, grid.own] = coef_in[:, grid.own]
    fold(coef, first, HALO, [x_before(base + a) for a in range(4)])
    fold(coef, bottom, HALO, [x_after(base + a) for a in range(4)])
    strip_coef[:, grid.own] = strip_coef_in[:, grid.own]
    start[:, :, pl.ds(TOP, 16)] = start_in[:, :, pl.ds(TOP, 16)]
    start[:, :, pl.ds(bottom - 16, 16)] = start_in[:, :, pl.ds(bottom - 16, 16)]
    for at in grid.middle:
        after_one[:, :, pl.ds(at, 8)] = after_one_in[:, :, pl.ds(at, 8)]
    blank = jnp.zeros((8 - HALO, LANES), jnp.float32)

    def corner(k, c, before):
        value = jnp.where(even_x == before, c_b[k, c], c_a[k, c])
        return jnp.concatenate([blank, value] if before else [value, blank], 0)

    unpack(0, 8, lambda k, c: corner(k, c, True), strip_coef, start, fields, groups)
    unpack(bottom, 8, lambda k, c: corner(k, c, False), strip_coef, start, fields, groups)

    def strip_body(g, carry):
        mine = flux.at[0]
        strip_velocities(grid.around, grid.outer, g, start, after_one, strip_coef, mine, edges, 0)
        strip_heights(grid.outer, g, after_one, strip_coef, mine)
        strip_velocities(grid.tiles, [], g, after_one, None, strip_coef, mine, edges, 4)
        return carry

    lax.fori_loop(0, groups, strip_body, 0)
    near = 24

    def body(i, carry):
        for k in range(WIDE):
            p = WIDE * i + k
            for c in range(fields):
                for at in (0, rows - near):
                    sea = coef[3, pl.ds(TOP + at, near)] != 0.0
                    value = probes[c, p, pl.ds(at, near)].astype(jnp.float32)
                    state[k, c, pl.ds(TOP + at, near)] = jnp.where(sea, value, 0.0)
                state[k, c, pl.ds(first, HALO)] = x_before(c * count + p)
                state[k, c, pl.ds(bottom, HALO)] = x_after(c * count + p)
                later[k, c, pl.ds(grid.middle[0], 8 * len(grid.middle))] = inner[p, c]
            for slot in range(4 * STEPS):
                for at in grid.around if slot < 4 else grid.tiles:
                    here = pl.ds(at, 8)
                    wraps_of[k, slot, here] = pltpu.roll(edges[slot, p // 8, here], turn_of(p), 1)

        for k in range(WIDE):

            def write_velocity(at, e_new, n_new):
                if at in grid.outer:
                    later[k, 1, pl.ds(at, 8)] = e_new
                    later[k, 2, pl.ds(at, 8)] = n_new

            def write_height(at, h_new):
                later[k, 0, pl.ds(at, 8)] = h_new

            def across(at):
                value, lane = flux[k, 1, pl.ds(at, 8)], lane_ids(8)
                up = jnp.where(lane == LANES - 1, 0.0, pltpu.roll(value, LANES - 1, 1))
                down = jnp.where(lane == 0, 0.0, pltpu.roll(value, 1, 1))
                return up - down + jnp.where(ends(), wraps_of[k, 3, pl.ds(at, 8)], 0.0)

            velocities(
                grid.around, lambda c: state.at[k, c], coef,
                lambda c, at, value: shifted(value, wraps_of[k, c, pl.ds(at, 8)]),
                flux.at[k], write_velocity,
            )
            heights(grid.outer, coef, across, flux.at[k], write_height)

        for k in range(WIDE):

            def row(c):
                return pl.multiple_of((c * count + WIDE * i + k) * tall, 8)

            def write_velocity(at, e_new, n_new):
                grid_state[pl.ds(row(1) + (at - first), 8)] = e_new
                grid_state[pl.ds(row(2) + (at - first), 8)] = n_new

            velocities(
                grid.tiles, lambda c: later.at[k, c], coef,
                lambda c, at, value: shifted(value, wraps_of[k, 4 + c, pl.ds(at, 8)]),
                flux.at[k], write_velocity,
            )
        flux_products(grid, flux, slope, weights)
        for k in range(WIDE):

            def row(c):
                return pl.multiple_of((c * count + WIDE * i + k) * tall, 8)

            def write_height(at, h_new):
                grid_state[pl.ds(row(0) + (at - first), 8)] = h_new

            def across(at):
                wrap = wraps_of[k, 7, pl.ds(at, 8)]
                return slope[pl.ds(k * grid.padded + at - first, 8)] + jnp.where(ends(), wrap, 0.0)

            heights(grid.tiles, coef, across, flux.at[k], write_height)
        return carry

    lax.fori_loop(0, count // WIDE, body, 0)

    total[...] = jnp.zeros_like(total)

    def gram_body(i, acc):
        c, block = i // (rows // BLOCK), lax.rem(i, rows // BLOCK)
        at = c * count * tall + block * BLOCK + HALO
        values = jnp.concatenate(
            [grid_state[pl.ds(at + x, count, stride=tall)] for x in range(BLOCK)], 1
        )
        top = values.astype(jnp.bfloat16)
        low = (values - top.astype(jnp.float32)).astype(jnp.bfloat16)
        both = jnp.concatenate([top, low], 0)
        halves[i] = both
        return acc + lax.dot_general(
            both, both, (((1,), (1,)), ((), ())), preferred_element_type=jnp.float32
        )

    acc = jnp.zeros((2 * count, 2 * count), jnp.float32)
    acc = lax.fori_loop(0, fields * rows // BLOCK, gram_body, acc, unroll=True)
    total[:, : 2 * count] = acc
    value = total[...]
    summed = value[:count] + value[count:]
    summed = summed + pltpu.roll(summed, LANES - count, 1)
    lane = lane_ids(count)
    summed = jnp.where(lane < count, summed, 0.0)
    out = summed[:8]
    for b in range(1, count // 8):
        out = out + pltpu.roll(summed[8 * b : 8 * b + 8], count * b, 1)
    gram[...] = out


def evolve(probes, known, *received):
    fields, count, rows, cols = probes.shape
    grid = Grid(rows)
    f32, groups, height = jnp.float32, count // 8, grid.height
    return pl.pallas_call(
        evolve_kernel,
        out_shape=(
            jax.ShapeDtypeStruct((fields * rows // BLOCK, 2 * count, BLOCK * cols), jnp.bfloat16),
            jax.ShapeDtypeStruct((8, LANES), f32),
        ),
        scratch_shapes=[
            pltpu.VMEM((4, height, LANES), f32),
            pltpu.VMEM((4, height, LANES), f32),
            pltpu.VMEM((fields, groups, height, LANES), f32),
            pltpu.VMEM((fields, groups, height, LANES), f32),
            pltpu.VMEM((4 * STEPS, groups, height, LANES), f32),
            pltpu.VMEM((2 * LANES, LANES), jnp.bfloat16),
            pltpu.VMEM((WIDE, 4 * STEPS, height, LANES), f32),
            pltpu.VMEM((WIDE, fields, height, LANES), f32),
            pltpu.VMEM((WIDE, fields, height, LANES), f32),
            pltpu.VMEM((WIDE, 3, height, LANES), f32),
            pltpu.VMEM((WIDE * grid.padded, LANES), f32),
            pltpu.VMEM((fields * count * grid.tall, LANES), f32),
            pltpu.VMEM((2 * count, LANES), f32),
        ],
        compiler_params=pltpu.CompilerParams(vmem_limit_bytes=30 * MIB),
        cost_estimate=pl.CostEstimate(flops=10**8, bytes_accessed=10**7, transcendentals=0),
        name="evolve_and_gram",
    )(probes, *known, *received)


def finish_kernel(scale, grams, halves, basis, triangle, grid_out, staged, sems):
    fields, count, rows, cols = staged.shape
    stride = grid_out.shape[0] // count
    summed = jnp.sum(grams[...], 0)
    lane = lane_ids(count)
    row_id = lax.broadcasted_iota(jnp.int32, (count, LANES), 0)
    gram = jnp.concatenate(
        [summed if b == 0 else pltpu.roll(summed, LANES - count * b, 1) for b in range(count // 8)],
        0,
    )
    work = jnp.where(lane < count, gram, jnp.where(lane == row_id + count, 1.0, 0.0))
    part = [work[8 * i : 8 * i + 8] for i in range(count // 8)]
    row8 = lax.broadcasted_iota(jnp.int32, (8, LANES), 0)

    def spread(value, k):
        return jnp.broadcast_to(value[:, k : k + 1], (8, LANES))

    for k in range(0, count, PIVOTS):
        span = range(PIVOTS)
        block = part[k // 8]
        pivot_rows = [jnp.broadcast_to(block[k % 8 + i : k % 8 + i + 1], (8, LANES)) for i in span]
        inner = [[spread(pivot_rows[j], k + i) for i in span] for j in span]
        columns = {r: [spread(part[r], k + i) for i in span] for r in range(k // 8, count // 8)}
        inverses = []
        for i in span:
            inverses.append(1.0 / inner[i][i])
            for j in range(i + 1, PIVOTS):
                ratio = inner[j][i] * inverses[i]
                pivot_rows[j] = pivot_rows[j] - ratio * pivot_rows[i]
                for m in range(i + 1, PIVOTS):
                    inner[j][m] = inner[j][m] - ratio * inner[i][m]
        for r, column in columns.items():
            ratios = []
            for i in span:
                left = column[i]
                for m in range(i):
                    left = left - ratios[m] * inner[m][i]
                left = left * inverses[i]
                if r == k // 8:
                    left = jnp.where(row8 > k % 8 + i, left, 0.0)
                ratios.append(left)
            for i in span:
                part[r] = part[r] - ratios[i] * pivot_rows[i]
    work = jnp.concatenate(part, 0)
    pivots = jnp.sum(jnp.where(lane == row_id, work, 0.0), 1, keepdims=True)
    work = work / jnp.sqrt(pivots)
    triangle[...] = jnp.where(lane >= row_id, work, 0.0)[:, :count] * (1.0 / scale)
    lower = (work * scale)[:, count : 2 * count]
    top = lower.astype(jnp.bfloat16)
    low = (lower - top.astype(jnp.float32)).astype(jnp.bfloat16)
    factor = jnp.concatenate([top, top, low], 1)

    copies = []
    for c in range(fields):

        def body(i, carry):
            both = halves[c * (rows // BLOCK) + i]
            stacked = jnp.concatenate([both, both[:count]], 0)
            out = jnp.dot(factor, stacked, preferred_element_type=jnp.float32)
            for x in range(BLOCK):
                at = BLOCK * i + x
                grid_out[pl.ds(at, count, stride=stride)] = out[:, x * cols : (x + 1) * cols]
            return carry

        lax.fori_loop(0, rows // BLOCK, body, 0, unroll=True)

        for part_of in range(PARTS):
            these = pl.ds(part_of * count // PARTS, count // PARTS)

            def store(q, carry):
                q = q + part_of * count // PARTS
                at = pl.multiple_of(q * stride, 8)
                staged[c, q] = grid_out[pl.ds(at, rows)].astype(jnp.bfloat16)
                return carry

            lax.fori_loop(0, count // PARTS, store, 0, unroll=4)
            copies.append(
                pltpu.make_async_copy(
                    staged.at[c, these], basis.at[c, these], sems.at[c * PARTS + part_of]
                )
            )
            copies[-1].start()
    for copy in copies:
        copy.wait()


def finish(grams, halves, shape, scale):
    fields, count, rows, cols = shape
    return pl.pallas_call(
        functools.partial(finish_kernel, scale),
        out_shape=(
            jax.ShapeDtypeStruct(shape, jnp.bfloat16),
            jax.ShapeDtypeStruct((count, count), jnp.float32),
        ),
        out_specs=(
            pl.BlockSpec(memory_space=pltpu.HBM),
            pl.BlockSpec(memory_space=pltpu.VMEM),
        ),
        scratch_shapes=[
            pltpu.VMEM((count * (rows + 8), cols), jnp.float32),
            pltpu.VMEM(shape, jnp.bfloat16),
            pltpu.SemaphoreType.DMA((fields * PARTS,)),
        ],
        compiler_params=pltpu.CompilerParams(vmem_limit_bytes=20 * MIB),
        name="factor_and_apply",
    )(grams, halves)


def first_pairs(size):
    return [(i, i ^ 1) for i in range(size)]


def second_pairs(size):
    return [(i, ((i + 1) ^ 1) - 1) for i in range(1, size - 1)]


def per_device(probes, depth, east_flow, north_flow, land_sea):
    fields, count, rows, cols = probes.shape
    nx, ny = lax.axis_size("gx"), lax.axis_size("gy")
    even_x = lax.rem(lax.axis_index("gx"), 2) == 0
    coefs = (depth, east_flow, north_flow, land_sea)
    x_a, x_b, to_a, to_b, held = pack(probes, *coefs)
    from_b = lax.ppermute(to_b, "gy", second_pairs(ny))
    from_a = lax.ppermute(to_a, "gy", first_pairs(ny))
    got_xb = lax.ppermute(x_b, "gx", second_pairs(nx))
    got_xa = lax.ppermute(x_a, "gx", first_pairs(nx))
    even_y = lax.rem(lax.axis_index("gy"), 2) == 0
    rows_of = (
        jnp.where(even_y, from_b, from_a),
        jnp.where(even_y, to_b, to_a),
        jnp.where(even_y, to_a, to_b),
        jnp.where(even_y, from_a, from_b),
    )
    low = jnp.stack([k[:, :HALO] for k in rows_of])
    high = jnp.stack([k[:, rows - HALO :] for k in rows_of])
    c_b = lax.ppermute(jnp.where(even_x, low, high), "gx", second_pairs(nx))
    c_a = lax.ppermute(jnp.where(even_x, high, low), "gx", first_pairs(nx))
    known = middle(held, coefs, to_a, to_b, from_a, from_b)
    halves, gram = evolve(held, known, got_xa, got_xb, c_a, c_b)
    devices = nx * ny
    grams = lax.all_to_all(
        jnp.broadcast_to(gram[None], (devices,) + gram.shape), ("gx", "gy"), 0, 0
    )
    scale = math.sqrt(fields * rows * nx * cols * ny)
    return finish(grams, halves, probes.shape, scale)


def solution(mesh):
    in_specs = (
        P(None, None, "gx", "gy"),
        P("gx", "gy"),
        P("gx", "gy"),
        P("gx", "gy"),
        P("gx", "gy"),
    )
    out_specs = (P(None, None, "gx", "gy"), P())
    return jax.shard_map(
        per_device, mesh=mesh, in_specs=in_specs, out_specs=out_specs, check_vma=False
    )
```

```python
import functools
import math

import jax
import jax.numpy as jnp
from jax import lax
from jax.experimental import pallas as pl
from jax.experimental.pallas import tpu as pltpu
from jax.sharding import PartitionSpec as P

STEPS = 2
HALO = 2 * STEPS
LANES = 128
TOP = 8

time_step = 0.3
coriolis = 0.5
gravity = 1.0

MIB = 1024 * 1024
BLOCK = 8
PARTS = 2
PIVOTS = 8
WIDE = 8


def lane_ids(rows):
    return lax.broadcasted_iota(jnp.int32, (rows, LANES), 1)


def in_hbm(arrays):
    return [pltpu.with_memory_space_constraint(v, pltpu.HBM) for v in arrays]


def pack_kernel(
    probes, depth, east_flow, north_flow, land_sea,
    x_a, x_b, y_a, y_b, held, coefs, mask, sems,
):
    fields, count, rows, _ = held.shape
    even_x = lax.rem(lax.axis_index("gx"), 2) == 0
    even_y = lax.rem(lax.axis_index("gy"), 2) == 0
    small = [
        pltpu.make_async_copy(source, target, sems.at[fields + i])
        for i, (source, target) in enumerate(
            ((land_sea, mask), (depth, coefs.at[0]), (east_flow, coefs.at[1]), (north_flow, coefs.at[2]))
        )
    ]
    large = [
        pltpu.make_async_copy(probes.at[c], held.at[c], sems.at[c]) for c in range(fields)
    ]
    for copy in small + large:
        copy.start()
    for copy in small:
        copy.wait()
    lane = lane_ids(rows)
    coefs[3] = mask[...].astype(jnp.float32)

    def place(index, low, high, value):
        at = HALO * index
        turned = pltpu.roll(value, at, 1) if index else value
        low = jnp.where((lane >= at) & (lane < at + HALO), turned, low)
        back = (at - HALO) % LANES
        high = jnp.where((lane >= back) & (lane < back + HALO), turned, high)
        return low, high

    def rows_out(at, value):
        low, high = value[:HALO], value[rows - HALO :]
        x_a[at] = jnp.where(even_x, high, low)
        x_b[at] = jnp.where(even_x, low, high)

    def columns_out(at, low, high):
        y_a[at] = jnp.where(even_y, high, low)
        y_b[at] = jnp.where(even_y, low, high)

    zero = jnp.zeros((rows, LANES), jnp.float32)
    low, high = zero, zero
    for a in range(4):
        value = coefs[a]
        rows_out(fields * count + a, value)
        low, high = place(a, low, high, value)
    columns_out(fields, low, high)
    for c in range(fields):
        large[c].wait()
        low, high = zero, zero
        for p in range(count):
            value = held[c, p].astype(jnp.float32) * coefs[3]
            rows_out(c * count + p, value)
            low, high = place(p, low, high, value)
        columns_out(c, low, high)


def pack(*arguments):
    probes = arguments[0]
    fields, count, rows, cols = probes.shape
    f32 = jnp.float32
    x_shape = jax.ShapeDtypeStruct((fields * count + 4, HALO, cols), f32)
    y_shape = jax.ShapeDtypeStruct((fields + 1, rows, LANES), f32)
    return pl.pallas_call(
        pack_kernel,
        in_specs=[pl.BlockSpec(memory_space=pltpu.HBM)] * 5,
        out_shape=(
            x_shape, x_shape, y_shape, y_shape,
            jax.ShapeDtypeStruct(probes.shape, probes.dtype),
        ),
        scratch_shapes=[
            pltpu.VMEM((4, rows, cols), f32),
            pltpu.VMEM((rows, cols), jnp.int32),
            pltpu.SemaphoreType.DMA((fields + 4,)),
        ],
        compiler_params=pltpu.CompilerParams(vmem_limit_bytes=16 * MIB),
        name="pack_edges",
    )(*in_hbm(arguments))


class Grid:
    def __init__(self, rows):
        self.rows = rows
        self.own = pl.ds(TOP, rows)
        self.bottom = TOP + rows
        self.first = TOP - HALO
        self.tall = rows + 2 * HALO
        self.tiles = [self.first + 8 * t for t in range(self.tall // 8)]
        self.padded = 16 * ((self.tall + 15) // 16)
        self.window = pl.ds(self.first, self.padded)
        self.height = self.padded + TOP
        self.middle = self.tiles[1:-1]
        self.outer = [self.tiles[0], self.tiles[-1]]
        self.around = [self.tiles[0], self.tiles[1], self.tiles[-2], self.tiles[-1]]


def fold(out, at, size, values):
    deep, east, north, sea = values
    half = 0.5 * time_step
    out[0, pl.ds(at, size)] = deep
    out[1, pl.ds(at, size)] = half * sea * east
    out[2, pl.ds(at, size)] = half * sea * north
    out[3, pl.ds(at, size)] = (half * gravity) * sea


def unpack(at, size, tile_of, strip_coef, strips, fields, groups):
    back = (HALO, 0, HALO, 0)
    lane = lane_ids(size)
    part = lax.rem(lane, 16) // HALO

    def gathered(plane, slot):
        out = None
        for k in range(4):
            index = (HALO * slot + lax.rem(lane, HALO) - back[k] + LANES) & (LANES - 1)
            picked = jnp.take_along_axis(tile_of(k, plane), index, axis=1)
            out = picked if out is None else jnp.where(part == k, picked, out)
        return out

    fold(strip_coef, at, size, [gathered(fields, jnp.full_like(lane, a)) for a in range(4)])
    for c in range(fields):
        for g in range(groups):
            strips[c, g, pl.ds(at, size)] = gathered(c, 8 * g + lane // 16)


def two(value):
    top = value.astype(jnp.bfloat16)
    return top, (value - top.astype(jnp.float32)).astype(jnp.bfloat16)


def shifted(value, wrap):
    lane = lane_ids(8)
    up = value if wrap is None else jnp.where(lane == 0, wrap, value)
    down = value if wrap is None else jnp.where(lane == LANES - 1, wrap, value)
    return pltpu.roll(up, LANES - 1, 1) - pltpu.roll(down, 1, 1)


def ends():
    lane = lane_ids(8)
    return (lane == 0) | (lane == LANES - 1)


def velocities(tiles, source, factors, differences, flux, write):
    for at in tiles:
        here, above, below = pl.ds(at, 8), pl.ds(at - 1, 8), pl.ds(at + 1, 8)
        deep, east, north, slope = [factors[a, here] for a in range(4)]
        h, e, n = [source(c)[here] for c in range(3)]
        xh, xe, xn = [source(c)[below] - source(c)[above] for c in range(3)]
        yh, ye, yn = [differences(c, at, v) for c, v in enumerate((h, e, n))]
        e_new = e + (time_step * coriolis) * n - (east * xe + north * ye + slope * xh)
        n_new = n - (time_step * coriolis) * e - (east * xn + north * yn + slope * yh)
        flux[0, here] = deep * e_new
        flux[1, here] = deep * n_new
        flux[2, here] = h - (east * xh + north * yh)
        write(at, e_new, n_new)


def heights(tiles, factors, across, flux, write):
    for at in tiles:
        here, above, below = pl.ds(at, 8), pl.ds(at - 1, 8), pl.ds(at + 1, 8)
        along = flux[0, below] - flux[0, above]
        write(at, flux[2, here] - factors[3, here] * (along + across(at)))


def plain(c, at, value):
    return shifted(value, None)


def keep(edges, slot, g, at, value):
    here = lax.rem(lane_ids(8), 16) == HALO
    edges[slot, g, pl.ds(at, 8)] = jnp.where(here, pltpu.roll(value, LANES - 8, 1), value)


def keep_flux(edges, slot, g, at, value):
    edges[slot, g, pl.ds(at, 8)] = lacking(value)


def lacking(value):
    here = lax.rem(lane_ids(8), 16) == HALO
    return jnp.where(here, -pltpu.roll(value, 1, 1), pltpu.roll(value, LANES - 9, 1))


def beside(value):
    here = lax.rem(lane_ids(8), 16) == HALO
    return jnp.where(here, value, pltpu.roll(value, LANES - 8, 1))


def keep_lacking(edges, g, at, now, strip_coef):
    here = pl.ds(at, 8)
    north, slope = beside(strip_coef[2, here]), beside(strip_coef[3, here])
    h, e, n = [lacking(now[c, g, here]) for c in range(3)]
    edges[0, g, here] = -north * h
    edges[1, g, here] = -north * e
    edges[2, g, here] = -(north * n + slope * h)


def strip_velocities(tiles, written, g, now, later, strip_coef, flux, edges, slot, alone=False):
    for at in tiles:
        if alone:
            keep_lacking(edges, g, at, now, strip_coef)
            continue
        for c in range(3):
            keep(edges, slot + c, g, at, now[c, g, pl.ds(at, 8)])

    def write(at, e_new, n_new):
        if later is not None and at in written:
            later[1, g, pl.ds(at, 8)] = e_new
            later[2, g, pl.ds(at, 8)] = n_new

    velocities(tiles, lambda c: now.at[c, g], strip_coef, plain, flux, write)
    for at in tiles:
        keep_flux(edges, slot + 3, g, at, flux[1, pl.ds(at, 8)])


def strip_heights(tiles, g, later, strip_coef, flux):
    def write(at, h_new):
        later[0, g, pl.ds(at, 8)] = h_new

    heights(tiles, strip_coef, lambda at: shifted(flux[1, pl.ds(at, 8)], None), flux, write)


def difference_weights():
    source = lax.broadcasted_iota(jnp.int32, (2 * LANES, LANES), 0) & (LANES - 1)
    target = lax.broadcasted_iota(jnp.int32, (2 * LANES, LANES), 1)
    plus = (source == target + 1).astype(jnp.float32)
    minus = (source == target - 1).astype(jnp.float32)
    return (plus - minus).astype(jnp.bfloat16)


def flux_products(grid, flux, slope, weights):
    for k in range(WIDE):
        slope[k * grid.padded : (k + 1) * grid.padded] = jnp.dot(
            jnp.concatenate(two(flux[k, 1, grid.window]), 1),
            weights[...],
            preferred_element_type=jnp.float32,
        )


def turn_of(p):
    return lax.rem(2 * LANES - 16 * lax.rem(p, 8) - HALO, LANES)


def alone_kernel(
    probes, depth, east_flow, north_flow, land_sea, first_e, first_n, first_h, coef,
    raw, mask, state, flux, sems,
):
    fields, count, rows, _ = probes.shape
    grid = Grid(rows)
    copies = [
        pltpu.make_async_copy(source, target, sems.at[i])
        for i, (source, target) in enumerate(
            ((land_sea, mask), (depth, raw.at[0]), (east_flow, raw.at[1]), (north_flow, raw.at[2]))
        )
    ]
    for copy in copies:
        copy.start()
    for copy in copies:
        copy.wait()
    raw[3] = mask[...].astype(jnp.float32)
    fold(coef, TOP, rows, [raw[a] for a in range(4)])
    lane = lane_ids(8)

    def differences(c, at, value):
        up = jnp.where(lane == LANES - 1, 0.0, pltpu.roll(value, LANES - 1, 1))
        return up - jnp.where(lane == 0, 0.0, pltpu.roll(value, 1, 1))

    def body(i, carry):
        for k in range(WIDE):
            p = WIDE * i + k
            for c in range(fields):
                state[k, c, grid.own] = probes[c, p].astype(jnp.float32) * raw[3]
        for k in range(WIDE):
            p = WIDE * i + k

            def write(at, e_new, n_new):
                first_e[p, pl.ds(at - grid.first, 8)] = e_new
                first_n[p, pl.ds(at - grid.first, 8)] = n_new
                first_h[p, pl.ds(at - grid.first, 8)] = flux[k, 2, pl.ds(at, 8)]

            velocities(
                grid.tiles, lambda c: state.at[k, c], coef, differences, flux.at[k], write
            )
        return carry

    lax.fori_loop(0, count // WIDE, body, 0)


def alone(probes, arguments):
    fields, count, rows, cols = probes.shape
    grid = Grid(rows)
    f32, height = jnp.float32, grid.height
    vmem, hbm = pl.BlockSpec(memory_space=pltpu.VMEM), pl.BlockSpec(memory_space=pltpu.HBM)
    one = jax.ShapeDtypeStruct((count, grid.tall, LANES), f32)
    return pl.pallas_call(
        alone_kernel,
        in_specs=[vmem] + [hbm] * 4,
        out_shape=(one, one, one, jax.ShapeDtypeStruct((4, height, LANES), f32)),
        scratch_shapes=[
            pltpu.VMEM((4, rows, cols), f32),
            pltpu.VMEM((rows, cols), jnp.int32),
            pltpu.VMEM((WIDE, fields, height, LANES), f32),
            pltpu.VMEM((WIDE, 3, height, LANES), f32),
            pltpu.SemaphoreType.DMA((4,)),
        ],
        compiler_params=pltpu.CompilerParams(vmem_limit_bytes=20 * MIB),
        cost_estimate=pl.CostEstimate(flops=10**8, bytes_accessed=10**7, transcendentals=0),
        name="first_velocities",
    )(probes, *in_hbm(arguments))


def corner_kernel(to_a, to_b, from_a, from_b, unused, c_a, c_b):
    planes, rows, _ = to_a.shape
    even_x = lax.rem(lax.axis_index("gx"), 2) == 0
    even_y = lax.rem(lax.axis_index("gy"), 2) == 0
    for k, (yes, no) in enumerate(((from_b, from_a), (to_b, to_a), (to_a, to_b), (from_a, from_b))):
        for c in range(planes):
            low = jnp.where(even_y, yes[c, pl.ds(0, HALO)], no[c, pl.ds(0, HALO)])
            end = pl.ds(rows - HALO, HALO)
            high = jnp.where(even_y, yes[c, end], no[c, end])
            c_a[k, c] = jnp.where(even_x, high, low)
            c_b[k, c] = jnp.where(even_x, low, high)


def corners(edges, before):
    shape = jax.ShapeDtypeStruct((4, edges[0].shape[0], HALO, LANES), jnp.float32)
    vmem, anywhere = pl.BlockSpec(memory_space=pltpu.VMEM), pl.BlockSpec(memory_space=pl.ANY)
    return pl.pallas_call(
        corner_kernel,
        in_specs=[vmem] * 4 + [anywhere],
        out_shape=(shape, shape),
        compiler_params=pltpu.CompilerParams(vmem_limit_bytes=8 * MIB),
        name="corner_rows",
    )(*edges, before)


def middle_kernel(
    first_e, first_n, first_h, coef, to_a, to_b, from_a, from_b,
    inner, strip_coef, start, after_one,
    edges, weights, wraps_of, flux, slope,
):
    count, fields = first_e.shape[0], to_a.shape[0] - 1
    rows = to_a.shape[1]
    grid = Grid(rows)
    groups = count // 8
    weights[...] = difference_weights()
    even_y = lax.rem(lax.axis_index("gy"), 2) == 0

    def kinds(k, *at):
        mine, theirs = (to_b, to_a) if k in (1, 2) else (from_b, from_a)
        if k in (2, 3):
            mine, theirs = theirs, mine
        return jnp.where(even_y, mine[at], theirs[at])

    for t in range(rows // 8):
        unpack(
            TOP + 8 * t, 8, lambda k, c: kinds(k, c, pl.ds(8 * t, 8)), strip_coef, start, fields, groups
        )

    def strip_body(g, carry):
        strip_velocities(
            grid.tiles, grid.middle, g, start, after_one, strip_coef, flux.at[0], edges, 0, True
        )
        strip_heights(grid.middle, g, after_one, strip_coef, flux.at[0])
        return carry

    lax.fori_loop(0, groups, strip_body, 0)

    def body(i, carry):
        for k in range(WIDE):
            p = WIDE * i + k
            for slot in range(4):
                for at in grid.tiles:
                    here = pl.ds(at, 8)
                    wraps_of[k, slot, here] = pltpu.roll(edges[slot, p // 8, here], turn_of(p), 1)
        for k in range(WIDE):
            p = WIDE * i + k
            for at in grid.tiles:
                here, there = pl.ds(at, 8), pl.ds(at - grid.first, 8)
                h, e, n = [
                    first[p, there] + jnp.where(ends(), wraps_of[k, c, here], 0.0)
                    for c, first in enumerate((first_h, first_e, first_n))
                ]
                deep = coef[0, here]
                flux[k, 0, here] = deep * e
                flux[k, 1, here] = deep * n
                flux[k, 2, here] = h
                if at in grid.middle:
                    inner[p, 1, pl.ds(at - grid.middle[0], 8)] = e
                    inner[p, 2, pl.ds(at - grid.middle[0], 8)] = n
        flux_products(grid, flux, slope, weights)
        for k in range(WIDE):
            p = WIDE * i + k

            def write_height(at, h_new):
                inner[p, 0, pl.ds(at - grid.middle[0], 8)] = h_new

            def across(at):
                wrap = wraps_of[k, 3, pl.ds(at, 8)]
                known = slope[pl.ds(k * grid.padded + at - grid.first, 8)]
                return known + jnp.where(ends(), wrap, 0.0)

            heights(grid.middle, coef, across, flux.at[k], write_height)
        return carry

    lax.fori_loop(0, count // WIDE, body, 0)


def middle(firsts, coef, *edges):
    fields, rows = edges[0].shape[0] - 1, edges[0].shape[1]
    count = firsts[0].shape[0]
    grid = Grid(rows)
    f32, groups, height = jnp.float32, count // 8, grid.height
    full = jax.ShapeDtypeStruct((fields, groups, height, LANES), f32)
    return pl.pallas_call(
        middle_kernel,
        out_shape=(
            jax.ShapeDtypeStruct((count, fields, 8 * len(grid.middle), LANES), f32),
            jax.ShapeDtypeStruct((4, height, LANES), f32),
            full,
            full,
        ),
        scratch_shapes=[
            pltpu.VMEM((4, groups, height, LANES), f32),
            pltpu.VMEM((2 * LANES, LANES), jnp.bfloat16),
            pltpu.VMEM((WIDE, 4, height, LANES), f32),
            pltpu.VMEM((WIDE, 3, height, LANES), f32),
            pltpu.VMEM((WIDE * grid.padded, LANES), f32),
        ],
        compiler_params=pltpu.CompilerParams(vmem_limit_bytes=24 * MIB),
        cost_estimate=pl.CostEstimate(flops=10**8, bytes_accessed=10**7, transcendentals=0),
        name="first_step",
    )(*firsts, coef, *edges)


def evolve_kernel(
    probes, inner, coef_in, strip_coef_in, start_in, after_one_in, x_a, x_b, c_a, c_b,
    halves, gram, coef, strip_coef, start, after_one, edges, weights,
    wraps_of, state, later, flux, slope, grid_state, total,
):
    fields, count, rows, _ = probes.shape
    grid = Grid(rows)
    groups = count // 8
    tall, first, bottom = grid.tall, grid.first, grid.bottom
    even_x = lax.rem(lax.axis_index("gx"), 2) == 0
    weights[...] = difference_weights()

    def x_before(i):
        return jnp.where(even_x, x_b[i], x_a[i])

    def x_after(i):
        return jnp.where(even_x, x_a[i], x_b[i])

    base = fields * count
    coef[:, grid.own] = coef_in[:, grid.own]
    fold(coef, first, HALO, [x_before(base + a) for a in range(4)])
    fold(coef, bottom, HALO, [x_after(base + a) for a in range(4)])
    strip_coef[:, grid.own] = strip_coef_in[:, grid.own]
    start[:, :, pl.ds(TOP, 16)] = start_in[:, :, pl.ds(TOP, 16)]
    start[:, :, pl.ds(bottom - 16, 16)] = start_in[:, :, pl.ds(bottom - 16, 16)]
    for at in grid.middle:
        after_one[:, :, pl.ds(at, 8)] = after_one_in[:, :, pl.ds(at, 8)]
    blank = jnp.zeros((8 - HALO, LANES), jnp.float32)

    def corner(k, c, before):
        value = jnp.where(even_x == before, c_b[k, c], c_a[k, c])
        return jnp.concatenate([blank, value] if before else [value, blank], 0)

    unpack(0, 8, lambda k, c: corner(k, c, True), strip_coef, start, fields, groups)
    unpack(bottom, 8, lambda k, c: corner(k, c, False), strip_coef, start, fields, groups)

    def strip_body(g, carry):
        mine = flux.at[0]
        strip_velocities(grid.around, grid.outer, g, start, after_one, strip_coef, mine, edges, 0)
        strip_heights(grid.outer, g, after_one, strip_coef, mine)
        strip_velocities(grid.tiles, [], g, after_one, None, strip_coef, mine, edges, 4)
        return carry

    lax.fori_loop(0, groups, strip_body, 0)
    near = 24

    def body(i, carry):
        for k in range(WIDE):
            p = WIDE * i + k
            for c in range(fields):
                for at in (0, rows - near):
                    sea = coef[3, pl.ds(TOP + at, near)] != 0.0
                    value = probes[c, p, pl.ds(at, near)].astype(jnp.float32)
                    state[k, c, pl.ds(TOP + at, near)] = jnp.where(sea, value, 0.0)
                state[k, c, pl.ds(first, HALO)] = x_before(c * count + p)
                state[k, c, pl.ds(bottom, HALO)] = x_after(c * count + p)
                later[k, c, pl.ds(grid.middle[0], 8 * len(grid.middle))] = inner[p, c]
            for slot in range(4 * STEPS):
                for at in grid.around if slot < 4 else grid.tiles:
                    here = pl.ds(at, 8)
                    wraps_of[k, slot, here] = pltpu.roll(edges[slot, p // 8, here], turn_of(p), 1)

        for k in range(WIDE):

            def write_velocity(at, e_new, n_new):
                if at in grid.outer:
                    later[k, 1, pl.ds(at, 8)] = e_new
                    later[k, 2, pl.ds(at, 8)] = n_new

            def write_height(at, h_new):
                later[k, 0, pl.ds(at, 8)] = h_new

            def across(at):
                value, lane = flux[k, 1, pl.ds(at, 8)], lane_ids(8)
                up = jnp.where(lane == LANES - 1, 0.0, pltpu.roll(value, LANES - 1, 1))
                down = jnp.where(lane == 0, 0.0, pltpu.roll(value, 1, 1))
                return up - down + jnp.where(ends(), wraps_of[k, 3, pl.ds(at, 8)], 0.0)

            velocities(
                grid.around, lambda c: state.at[k, c], coef,
                lambda c, at, value: shifted(value, wraps_of[k, c, pl.ds(at, 8)]),
                flux.at[k], write_velocity,
            )
            heights(grid.outer, coef, across, flux.at[k], write_height)

        for k in range(WIDE):

            def row(c):
                return pl.multiple_of((c * count + WIDE * i + k) * tall, 8)

            def write_velocity(at, e_new, n_new):
                grid_state[pl.ds(row(1) + (at - first), 8)] = e_new
                grid_state[pl.ds(row(2) + (at - first), 8)] = n_new

            velocities(
                grid.tiles, lambda c: later.at[k, c], coef,
                lambda c, at, value: shifted(value, wraps_of[k, 4 + c, pl.ds(at, 8)]),
                flux.at[k], write_velocity,
            )
        flux_products(grid, flux, slope, weights)
        for k in range(WIDE):

            def row(c):
                return pl.multiple_of((c * count + WIDE * i + k) * tall, 8)

            def write_height(at, h_new):
                grid_state[pl.ds(row(0) + (at - first), 8)] = h_new

            def across(at):
                wrap = wraps_of[k, 7, pl.ds(at, 8)]
                return slope[pl.ds(k * grid.padded + at - first, 8)] + jnp.where(ends(), wrap, 0.0)

            heights(grid.tiles, coef, across, flux.at[k], write_height)
        return carry

    lax.fori_loop(0, count // WIDE, body, 0)

    total[...] = jnp.zeros_like(total)

    def gram_body(i, acc):
        c, block = i // (rows // BLOCK), lax.rem(i, rows // BLOCK)
        at = c * count * tall + block * BLOCK + HALO
        values = jnp.concatenate(
            [grid_state[pl.ds(at + x, count, stride=tall)] for x in range(BLOCK)], 1
        )
        top = values.astype(jnp.bfloat16)
        low = (values - top.astype(jnp.float32)).astype(jnp.bfloat16)
        both = jnp.concatenate([top, low], 0)
        halves[i] = both
        return acc + lax.dot_general(
            both, both, (((1,), (1,)), ((), ())), preferred_element_type=jnp.float32
        )

    acc = jnp.zeros((2 * count, 2 * count), jnp.float32)
    acc = lax.fori_loop(0, fields * rows // BLOCK, gram_body, acc, unroll=True)
    total[:, : 2 * count] = acc
    value = total[...]
    summed = value[:count] + value[count:]
    summed = summed + pltpu.roll(summed, LANES - count, 1)
    lane = lane_ids(count)
    summed = jnp.where(lane < count, summed, 0.0)
    out = summed[:8]
    for b in range(1, count // 8):
        out = out + pltpu.roll(summed[8 * b : 8 * b + 8], count * b, 1)
    gram[...] = out


def evolve(probes, known, *received):
    fields, count, rows, cols = probes.shape
    grid = Grid(rows)
    f32, groups, height = jnp.float32, count // 8, grid.height
    return pl.pallas_call(
        evolve_kernel,
        out_shape=(
            jax.ShapeDtypeStruct((fields * rows // BLOCK, 2 * count, BLOCK * cols), jnp.bfloat16),
            jax.ShapeDtypeStruct((8, LANES), f32),
        ),
        scratch_shapes=[
            pltpu.VMEM((4, height, LANES), f32),
            pltpu.VMEM((4, height, LANES), f32),
            pltpu.VMEM((fields, groups, height, LANES), f32),
            pltpu.VMEM((fields, groups, height, LANES), f32),
            pltpu.VMEM((4 * STEPS, groups, height, LANES), f32),
            pltpu.VMEM((2 * LANES, LANES), jnp.bfloat16),
            pltpu.VMEM((WIDE, 4 * STEPS, height, LANES), f32),
            pltpu.VMEM((WIDE, fields, height, LANES), f32),
            pltpu.VMEM((WIDE, fields, height, LANES), f32),
            pltpu.VMEM((WIDE, 3, height, LANES), f32),
            pltpu.VMEM((WIDE * grid.padded, LANES), f32),
            pltpu.VMEM((fields * count * grid.tall, LANES), f32),
            pltpu.VMEM((2 * count, LANES), f32),
        ],
        compiler_params=pltpu.CompilerParams(vmem_limit_bytes=30 * MIB),
        cost_estimate=pl.CostEstimate(flops=10**8, bytes_accessed=10**7, transcendentals=0),
        name="evolve_and_gram",
    )(probes, *known, *received)


def finish_kernel(scale, grams, halves, basis, triangle, grid_out, staged, sems):
    fields, count, rows, cols = staged.shape
    stride = grid_out.shape[0] // count
    summed = jnp.sum(grams[...], 0)
    lane = lane_ids(count)
    row_id = lax.broadcasted_iota(jnp.int32, (count, LANES), 0)
    gram = jnp.concatenate(
        [summed if b == 0 else pltpu.roll(summed, LANES - count * b, 1) for b in range(count // 8)],
        0,
    )
    work = jnp.where(lane < count, gram, jnp.where(lane == row_id + count, 1.0, 0.0))
    part = [work[8 * i : 8 * i + 8] for i in range(count // 8)]
    row8 = lax.broadcasted_iota(jnp.int32, (8, LANES), 0)

    def spread(value, k):
        return jnp.broadcast_to(value[:, k : k + 1], (8, LANES))

    for k in range(0, count, PIVOTS):
        span = range(PIVOTS)
        block = part[k // 8]
        pivot_rows = [jnp.broadcast_to(block[k % 8 + i : k % 8 + i + 1], (8, LANES)) for i in span]
        inner = [[spread(pivot_rows[j], k + i) for i in span] for j in span]
        columns = {r: [spread(part[r], k + i) for i in span] for r in range(k // 8, count // 8)}
        inverses = []
        for i in span:
            inverses.append(1.0 / inner[i][i])
            for j in range(i + 1, PIVOTS):
                ratio = inner[j][i] * inverses[i]
                pivot_rows[j] = pivot_rows[j] - ratio * pivot_rows[i]
                for m in range(i + 1, PIVOTS):
                    inner[j][m] = inner[j][m] - ratio * inner[i][m]
        for r, column in columns.items():
            ratios = []
            for i in span:
                left = column[i]
                for m in range(i):
                    left = left - ratios[m] * inner[m][i]
                left = left * inverses[i]
                if r == k // 8:
                    left = jnp.where(row8 > k % 8 + i, left, 0.0)
                ratios.append(left)
            for i in span:
                part[r] = part[r] - ratios[i] * pivot_rows[i]
    work = jnp.concatenate(part, 0)
    pivots = jnp.sum(jnp.where(lane == row_id, work, 0.0), 1, keepdims=True)
    work = work / jnp.sqrt(pivots)
    triangle[...] = jnp.where(lane >= row_id, work, 0.0)[:, :count] * (1.0 / scale)
    lower = (work * scale)[:, count : 2 * count]
    top = lower.astype(jnp.bfloat16)
    low = (lower - top.astype(jnp.float32)).astype(jnp.bfloat16)
    factor = jnp.concatenate([top, top, low], 1)

    copies = []
    for c in range(fields):

        def body(i, carry):
            both = halves[c * (rows // BLOCK) + i]
            stacked = jnp.concatenate([both, both[:count]], 0)
            out = jnp.dot(factor, stacked, preferred_element_type=jnp.float32)
            for x in range(BLOCK):
                at = BLOCK * i + x
                grid_out[pl.ds(at, count, stride=stride)] = out[:, x * cols : (x + 1) * cols]
            return carry

        lax.fori_loop(0, rows // BLOCK, body, 0, unroll=True)

        for part_of in range(PARTS):
            these = pl.ds(part_of * count // PARTS, count // PARTS)

            def store(q, carry):
                q = q + part_of * count // PARTS
                at = pl.multiple_of(q * stride, 8)
                staged[c, q] = grid_out[pl.ds(at, rows)].astype(jnp.bfloat16)
                return carry

            lax.fori_loop(0, count // PARTS, store, 0, unroll=4)
            copies.append(
                pltpu.make_async_copy(
                    staged.at[c, these], basis.at[c, these], sems.at[c * PARTS + part_of]
                )
            )
            copies[-1].start()
    for copy in copies:
        copy.wait()


def finish(grams, halves, shape, scale):
    fields, count, rows, cols = shape
    return pl.pallas_call(
        functools.partial(finish_kernel, scale),
        out_shape=(
            jax.ShapeDtypeStruct(shape, jnp.bfloat16),
            jax.ShapeDtypeStruct((count, count), jnp.float32),
        ),
        out_specs=(
            pl.BlockSpec(memory_space=pltpu.HBM),
            pl.BlockSpec(memory_space=pltpu.VMEM),
        ),
        scratch_shapes=[
            pltpu.VMEM((count * (rows + 8), cols), jnp.float32),
            pltpu.VMEM(shape, jnp.bfloat16),
            pltpu.SemaphoreType.DMA((fields * PARTS,)),
        ],
        compiler_params=pltpu.CompilerParams(vmem_limit_bytes=20 * MIB),
        name="factor_and_apply",
    )(grams, halves)


def first_pairs(size):
    return [(i, i ^ 1) for i in range(size)]


def second_pairs(size):
    return [(i, ((i + 1) ^ 1) - 1) for i in range(1, size - 1)]


def per_device(probes, depth, east_flow, north_flow, land_sea):
    fields, count, rows, cols = probes.shape
    nx, ny = lax.axis_size("gx"), lax.axis_size("gy")
    coefs = (depth, east_flow, north_flow, land_sea)
    x_a, x_b, to_a, to_b, held = pack(probes, *coefs)
    from_b = lax.ppermute(to_b, "gy", second_pairs(ny))
    from_a = lax.ppermute(to_a, "gy", first_pairs(ny))
    got_xb = lax.ppermute(x_b, "gx", second_pairs(nx))
    got_xa = lax.ppermute(x_a, "gx", first_pairs(nx))
    *firsts, coef = alone(held, coefs)
    low_high = corners((to_a, to_b, from_a, from_b), firsts[0])
    c_b = lax.ppermute(low_high[1], "gx", second_pairs(nx))
    c_a = lax.ppermute(low_high[0], "gx", first_pairs(nx))
    inner, *strip_arrays = middle(firsts, coef, to_a, to_b, from_a, from_b)
    halves, gram = evolve(held, (inner, coef, *strip_arrays), got_xa, got_xb, c_a, c_b)
    devices = nx * ny
    grams = lax.all_to_all(
        jnp.broadcast_to(gram[None], (devices,) + gram.shape), ("gx", "gy"), 0, 0
    )
    scale = math.sqrt(fields * rows * nx * cols * ny)
    return finish(grams, halves, probes.shape, scale)


def solution(mesh):
    in_specs = (
        P(None, None, "gx", "gy"),
        P("gx", "gy"),
        P("gx", "gy"),
        P("gx", "gy"),
        P("gx", "gy"),
    )
    out_specs = (P(None, None, "gx", "gy"), P())
    return jax.shard_map(
        per_device, mesh=mesh, in_specs=in_specs, out_specs=out_specs, check_vma=False
    )
```

```python
import functools
import math

import jax
import jax.numpy as jnp
from jax import lax
from jax.experimental import pallas as pl
from jax.experimental.pallas import tpu as pltpu
from jax.sharding import PartitionSpec as P

STEPS = 2
HALO = 2 * STEPS
LANES = 128
TOP = 8

time_step = 0.3
coriolis = 0.5
gravity = 1.0

MIB = 1024 * 1024
BLOCK = 8
PARTS = 2
FIRST = (0, 1)
SECOND = (0, 1, 2)
PIVOTS = 8
WIDE = 8


def lane_ids(rows):
    return lax.broadcasted_iota(jnp.int32, (rows, LANES), 1)


def in_hbm(arrays):
    return [pltpu.with_memory_space_constraint(v, pltpu.HBM) for v in arrays]


def pack_kernel(
    probes, depth, east_flow, north_flow, land_sea,
    x_a, x_b, y_a, y_b, held, coefs, mask, sems,
):
    fields, count, rows, _ = held.shape
    even_x = lax.rem(lax.axis_index("gx"), 2) == 0
    even_y = lax.rem(lax.axis_index("gy"), 2) == 0
    small = [
        pltpu.make_async_copy(source, target, sems.at[fields + i])
        for i, (source, target) in enumerate(
            ((land_sea, mask), (depth, coefs.at[0]), (east_flow, coefs.at[1]), (north_flow, coefs.at[2]))
        )
    ]
    large = [
        pltpu.make_async_copy(probes.at[c], held.at[c], sems.at[c]) for c in range(fields)
    ]
    for copy in small + large:
        copy.start()
    for copy in small:
        copy.wait()
    lane = lane_ids(rows)
    coefs[3] = mask[...].astype(jnp.float32)

    def place(index, low, high, value):
        at = HALO * index
        turned = pltpu.roll(value, at, 1) if index else value
        low = jnp.where((lane >= at) & (lane < at + HALO), turned, low)
        back = (at - HALO) % LANES
        high = jnp.where((lane >= back) & (lane < back + HALO), turned, high)
        return low, high

    def rows_out(at, value):
        low, high = value[:HALO], value[rows - HALO :]
        x_a[at] = jnp.where(even_x, high, low)
        x_b[at] = jnp.where(even_x, low, high)

    def columns_out(at, low, high):
        y_a[at] = jnp.where(even_y, high, low)
        y_b[at] = jnp.where(even_y, low, high)

    zero = jnp.zeros((rows, LANES), jnp.float32)
    low, high = zero, zero
    for a in range(4):
        value = coefs[a]
        rows_out(fields * count + a, value)
        low, high = place(a, low, high, value)
    columns_out(fields, low, high)
    for c in range(fields):
        large[c].wait()
        low, high = zero, zero
        for p in range(count):
            value = held[c, p].astype(jnp.float32) * coefs[3]
            rows_out(c * count + p, value)
            low, high = place(p, low, high, value)
        columns_out(c, low, high)


def pack(*arguments):
    probes = arguments[0]
    fields, count, rows, cols = probes.shape
    f32 = jnp.float32
    x_shape = jax.ShapeDtypeStruct((fields * count + 4, HALO, cols), f32)
    y_shape = jax.ShapeDtypeStruct((fields + 1, rows, LANES), f32)
    return pl.pallas_call(
        pack_kernel,
        in_specs=[pl.BlockSpec(memory_space=pltpu.HBM)] * 5,
        out_shape=(
            x_shape, x_shape, y_shape, y_shape,
            jax.ShapeDtypeStruct(probes.shape, probes.dtype),
        ),
        scratch_shapes=[
            pltpu.VMEM((4, rows, cols), f32),
            pltpu.VMEM((rows, cols), jnp.int32),
            pltpu.SemaphoreType.DMA((fields + 4,)),
        ],
        compiler_params=pltpu.CompilerParams(vmem_limit_bytes=16 * MIB),
        name="pack_edges",
    )(*in_hbm(arguments))


class Grid:
    def __init__(self, rows):
        self.rows = rows
        self.own = pl.ds(TOP, rows)
        self.bottom = TOP + rows
        self.first = TOP - HALO
        self.tall = rows + 2 * HALO
        self.tiles = [self.first + 8 * t for t in range(self.tall // 8)]
        self.padded = 16 * ((self.tall + 15) // 16)
        self.window = pl.ds(self.first, self.padded)
        self.height = self.padded + TOP
        self.middle = self.tiles[1:-1]
        self.outer = [self.tiles[0], self.tiles[-1]]
        self.beside_outer = [self.tiles[1], self.tiles[-2]]


def fold(out, at, size, values):
    deep, east, north, sea = values
    half = 0.5 * time_step
    out[0, pl.ds(at, size)] = deep
    out[1, pl.ds(at, size)] = half * sea * east
    out[2, pl.ds(at, size)] = half * sea * north
    out[3, pl.ds(at, size)] = (half * gravity) * sea


def unpack(at, size, tile_of, strip_coef, strips, fields, groups):
    back = (HALO, 0, HALO, 0)
    lane = lane_ids(size)
    part = lax.rem(lane, 16) // HALO

    def gathered(plane, slot):
        out = None
        for k in range(4):
            index = (HALO * slot + lax.rem(lane, HALO) - back[k] + LANES) & (LANES - 1)
            picked = jnp.take_along_axis(tile_of(k, plane), index, axis=1)
            out = picked if out is None else jnp.where(part == k, picked, out)
        return out

    fold(strip_coef, at, size, [gathered(fields, jnp.full_like(lane, a)) for a in range(4)])
    for c in range(fields):
        for g in range(groups):
            strips[c, g, pl.ds(at, size)] = gathered(c, 8 * g + lane // 16)


def two(value):
    top = value.astype(jnp.bfloat16)
    return top, (value - top.astype(jnp.float32)).astype(jnp.bfloat16)


def shifted(value, wrap):
    lane = lane_ids(8)
    up = value if wrap is None else jnp.where(lane == 0, wrap, value)
    down = value if wrap is None else jnp.where(lane == LANES - 1, wrap, value)
    return pltpu.roll(up, LANES - 1, 1) - pltpu.roll(down, 1, 1)


def ends():
    lane = lane_ids(8)
    return (lane == 0) | (lane == LANES - 1)


def velocities(tiles, source, factors, differences, flux, write):
    for at in tiles:
        here, above, below = pl.ds(at, 8), pl.ds(at - 1, 8), pl.ds(at + 1, 8)
        deep, east, north, slope = [factors[a, here] for a in range(4)]
        h, e, n = [source(c)[here] for c in range(3)]
        xh, xe, xn = [source(c)[below] - source(c)[above] for c in range(3)]
        yh, ye, yn = [differences(c, at, v) for c, v in enumerate((h, e, n))]
        e_new = e + (time_step * coriolis) * n - (east * xe + north * ye + slope * xh)
        n_new = n - (time_step * coriolis) * e - (east * xn + north * yn + slope * yh)
        flux[0, here] = deep * e_new
        flux[1, here] = deep * n_new
        flux[2, here] = h - (east * xh + north * yh)
        write(at, e_new, n_new)


def heights(tiles, factors, across, flux, write):
    for at in tiles:
        here, above, below = pl.ds(at, 8), pl.ds(at - 1, 8), pl.ds(at + 1, 8)
        along = flux[0, below] - flux[0, above]
        write(at, flux[2, here] - factors[3, here] * (along + across(at)))


def plain(c, at, value):
    return shifted(value, None)


def keep(edges, slot, g, at, value):
    here = lax.rem(lane_ids(8), 16) == HALO
    edges[slot, g, pl.ds(at, 8)] = jnp.where(here, pltpu.roll(value, LANES - 8, 1), value)


def keep_flux(edges, slot, g, at, value):
    edges[slot, g, pl.ds(at, 8)] = lacking(value)


def lacking(value):
    here = lax.rem(lane_ids(8), 16) == HALO
    return jnp.where(here, -pltpu.roll(value, 1, 1), pltpu.roll(value, LANES - 9, 1))


def beside(value):
    here = lax.rem(lane_ids(8), 16) == HALO
    return jnp.where(here, value, pltpu.roll(value, LANES - 8, 1))


def keep_lacking(edges, g, at, now, strip_coef):
    here = pl.ds(at, 8)
    north, slope = beside(strip_coef[2, here]), beside(strip_coef[3, here])
    h, e, n = [lacking(now[c, g, here]) for c in range(3)]
    edges[0, g, here] = -north * h
    edges[1, g, here] = -north * e
    edges[2, g, here] = -(north * n + slope * h)


def strip_velocities(tiles, written, g, now, later, strip_coef, flux, edges, slot, alone=False, lack=()):
    for at in tiles:
        if alone:
            keep_lacking(edges, g, at, now, strip_coef)
            continue
        for c in range(3):
            save = keep_flux if c in lack else keep
            save(edges, slot + c, g, at, now[c, g, pl.ds(at, 8)])

    def write(at, e_new, n_new):
        if later is not None and at in written:
            later[1, g, pl.ds(at, 8)] = e_new
            later[2, g, pl.ds(at, 8)] = n_new

    velocities(tiles, lambda c: now.at[c, g], strip_coef, plain, flux, write)
    for at in tiles:
        keep_flux(edges, slot + 3, g, at, flux[1, pl.ds(at, 8)])


def strip_heights(tiles, g, later, strip_coef, flux):
    def write(at, h_new):
        later[0, g, pl.ds(at, 8)] = h_new

    heights(tiles, strip_coef, lambda at: shifted(flux[1, pl.ds(at, 8)], None), flux, write)


def difference_weights():
    source = lax.broadcasted_iota(jnp.int32, (2 * LANES, LANES), 0) & (LANES - 1)
    target = lax.broadcasted_iota(jnp.int32, (2 * LANES, LANES), 1)
    plus = (source == target + 1).astype(jnp.float32)
    minus = (source == target - 1).astype(jnp.float32)
    return (plus - minus).astype(jnp.bfloat16)


def field_products(grid, source, slope, weights, chosen):
    for j, c in enumerate(chosen):
        for k in range(WIDE):
            slope[j, k * grid.padded : (k + 1) * grid.padded] = jnp.dot(
                jnp.concatenate(two(source[k, c, grid.window]), 1),
                weights[...],
                preferred_element_type=jnp.float32,
            )


def flux_products(grid, flux, slope, weights):
    for k in range(WIDE):
        slope[k * grid.padded : (k + 1) * grid.padded] = jnp.dot(
            jnp.concatenate(two(flux[k, 1, grid.window]), 1),
            weights[...],
            preferred_element_type=jnp.float32,
        )


def turn_of(p):
    return lax.rem(2 * LANES - 16 * lax.rem(p, 8) - HALO, LANES)


def alone_kernel(
    probes, depth, east_flow, north_flow, land_sea, first_e, first_n, first_h, coef,
    raw, mask, state, flux, slope, weights, sems,
):
    fields, count, rows, _ = probes.shape
    grid = Grid(rows)
    copies = [
        pltpu.make_async_copy(source, target, sems.at[i])
        for i, (source, target) in enumerate(
            ((land_sea, mask), (depth, raw.at[0]), (east_flow, raw.at[1]), (north_flow, raw.at[2]))
        )
    ]
    for copy in copies:
        copy.start()
    for copy in copies:
        copy.wait()
    raw[3] = mask[...].astype(jnp.float32)
    fold(coef, TOP, rows, [raw[a] for a in range(4)])
    lane = lane_ids(8)
    weights[...] = difference_weights()[:LANES]

    def differences(k, c, at, value):
        if c in FIRST:
            return slope[FIRST.index(c), pl.ds(k * grid.padded + at - grid.first, 8)]
        up = jnp.where(lane == LANES - 1, 0.0, pltpu.roll(value, LANES - 1, 1))
        return up - jnp.where(lane == 0, 0.0, pltpu.roll(value, 1, 1))

    def body(i, carry):
        for k in range(WIDE):
            p = WIDE * i + k
            for c in range(fields):
                state[k, c, grid.own] = probes[c, p].astype(jnp.float32) * raw[3]
        for j, c in enumerate(FIRST):
            for k in range(WIDE):
                slope[j, k * grid.padded : (k + 1) * grid.padded] = jnp.dot(
                    state[k, c, grid.window].astype(jnp.bfloat16),
                    weights[...],
                    preferred_element_type=jnp.float32,
                )
        for k in range(WIDE):
            p = WIDE * i + k

            def write(at, e_new, n_new):
                first_e[p, pl.ds(at - grid.first, 8)] = e_new
                first_n[p, pl.ds(at - grid.first, 8)] = n_new
                first_h[p, pl.ds(at - grid.first, 8)] = flux[k, 2, pl.ds(at, 8)]

            velocities(
                grid.tiles, lambda c: state.at[k, c], coef,
                functools.partial(differences, k), flux.at[k], write,
            )
        return carry

    lax.fori_loop(0, count // WIDE, body, 0)


def alone(probes, arguments):
    fields, count, rows, cols = probes.shape
    grid = Grid(rows)
    f32, height = jnp.float32, grid.height
    vmem, hbm = pl.BlockSpec(memory_space=pltpu.VMEM), pl.BlockSpec(memory_space=pltpu.HBM)
    one = jax.ShapeDtypeStruct((count, grid.tall, LANES), f32)
    return pl.pallas_call(
        alone_kernel,
        in_specs=[vmem] + [hbm] * 4,
        out_shape=(one, one, one, jax.ShapeDtypeStruct((4, height, LANES), f32)),
        scratch_shapes=[
            pltpu.VMEM((4, rows, cols), f32),
            pltpu.VMEM((rows, cols), jnp.int32),
            pltpu.VMEM((WIDE, fields, height, LANES), f32),
            pltpu.VMEM((WIDE, 3, height, LANES), f32),
            pltpu.VMEM((max(len(FIRST), 1), WIDE * grid.padded, LANES), f32),
            pltpu.VMEM((LANES, LANES), jnp.bfloat16),
            pltpu.SemaphoreType.DMA((4,)),
        ],
        compiler_params=pltpu.CompilerParams(vmem_limit_bytes=20 * MIB),
        cost_estimate=pl.CostEstimate(flops=10**8, bytes_accessed=10**7, transcendentals=0),
        name="first_velocities",
    )(probes, *in_hbm(arguments))


def corner_kernel(to_a, to_b, from_a, from_b, unused, c_a, c_b):
    planes, rows, _ = to_a.shape
    even_x = lax.rem(lax.axis_index("gx"), 2) == 0
    even_y = lax.rem(lax.axis_index("gy"), 2) == 0
    for k, (yes, no) in enumerate(((from_b, from_a), (to_b, to_a), (to_a, to_b), (from_a, from_b))):
        for c in range(planes):
            low = jnp.where(even_y, yes[c, pl.ds(0, HALO)], no[c, pl.ds(0, HALO)])
            end = pl.ds(rows - HALO, HALO)
            high = jnp.where(even_y, yes[c, end], no[c, end])
            c_a[k, c] = jnp.where(even_x, high, low)
            c_b[k, c] = jnp.where(even_x, low, high)


def corners(edges, before):
    shape = jax.ShapeDtypeStruct((4, edges[0].shape[0], HALO, LANES), jnp.float32)
    vmem, anywhere = pl.BlockSpec(memory_space=pltpu.VMEM), pl.BlockSpec(memory_space=pl.ANY)
    return pl.pallas_call(
        corner_kernel,
        in_specs=[vmem] * 4 + [anywhere],
        out_shape=(shape, shape),
        compiler_params=pltpu.CompilerParams(vmem_limit_bytes=8 * MIB),
        name="corner_rows",
    )(*edges, before)


def middle_kernel(
    first_e, first_n, first_h, coef, to_a, to_b, from_a, from_b,
    inner, strip_coef, start, after_one,
    edges, weights, wraps_of, flux, slope,
):
    count, fields = first_e.shape[0], to_a.shape[0] - 1
    rows = to_a.shape[1]
    grid = Grid(rows)
    groups = count // 8
    weights[...] = difference_weights()
    even_y = lax.rem(lax.axis_index("gy"), 2) == 0

    def kinds(k, *at):
        mine, theirs = (to_b, to_a) if k in (1, 2) else (from_b, from_a)
        if k in (2, 3):
            mine, theirs = theirs, mine
        return jnp.where(even_y, mine[at], theirs[at])

    for t in range(rows // 8):
        unpack(
            TOP + 8 * t, 8, lambda k, c: kinds(k, c, pl.ds(8 * t, 8)), strip_coef, start, fields, groups
        )

    def strip_body(g, carry):
        strip_velocities(
            grid.tiles, grid.middle, g, start, after_one, strip_coef, flux.at[0], edges, 0, True
        )
        strip_heights(grid.middle, g, after_one, strip_coef, flux.at[0])
        return carry

    lax.fori_loop(0, groups, strip_body, 0)

    def body(i, carry):
        for k in range(WIDE):
            p = WIDE * i + k
            for slot in range(4):
                for at in grid.tiles:
                    here = pl.ds(at, 8)
                    wraps_of[k, slot, here] = pltpu.roll(edges[slot, p // 8, here], turn_of(p), 1)
        for k in range(WIDE):
            p = WIDE * i + k
            for at in grid.tiles:
                here, there = pl.ds(at, 8), pl.ds(at - grid.first, 8)
                h, e, n = [
                    first[p, there] + jnp.where(ends(), wraps_of[k, c, here], 0.0)
                    for c, first in enumerate((first_h, first_e, first_n))
                ]
                deep = coef[0, here]
                flux[k, 0, here] = deep * e
                flux[k, 1, here] = deep * n
                flux[k, 2, here] = h
                if at in grid.middle:
                    inner[p, 1, pl.ds(at - grid.middle[0], 8)] = e
                    inner[p, 2, pl.ds(at - grid.middle[0], 8)] = n
        flux_products(grid, flux, slope, weights)
        for k in range(WIDE):
            p = WIDE * i + k

            def write_height(at, h_new):
                inner[p, 0, pl.ds(at - grid.middle[0], 8)] = h_new

            def across(at):
                wrap = wraps_of[k, 3, pl.ds(at, 8)]
                known = slope[pl.ds(k * grid.padded + at - grid.first, 8)]
                return known + jnp.where(ends(), wrap, 0.0)

            heights(grid.middle, coef, across, flux.at[k], write_height)
        return carry

    lax.fori_loop(0, count // WIDE, body, 0)


def middle(firsts, coef, *edges):
    fields, rows = edges[0].shape[0] - 1, edges[0].shape[1]
    count = firsts[0].shape[0]
    grid = Grid(rows)
    f32, groups, height = jnp.float32, count // 8, grid.height
    full = jax.ShapeDtypeStruct((fields, groups, height, LANES), f32)
    return pl.pallas_call(
        middle_kernel,
        out_shape=(
            jax.ShapeDtypeStruct((count, fields, 8 * len(grid.middle), LANES), f32),
            jax.ShapeDtypeStruct((4, height, LANES), f32),
            full,
            full,
        ),
        scratch_shapes=[
            pltpu.VMEM((4, groups, height, LANES), f32),
            pltpu.VMEM((2 * LANES, LANES), jnp.bfloat16),
            pltpu.VMEM((WIDE, 4, height, LANES), f32),
            pltpu.VMEM((WIDE, 3, height, LANES), f32),
            pltpu.VMEM((WIDE * grid.padded, LANES), f32),
        ],
        compiler_params=pltpu.CompilerParams(vmem_limit_bytes=24 * MIB),
        cost_estimate=pl.CostEstimate(flops=10**8, bytes_accessed=10**7, transcendentals=0),
        name="first_step",
    )(*firsts, coef, *edges)


def evolve_kernel(
    probes, inner, coef_in, strip_coef_in, start_in, after_one_in, x_a, x_b, c_a, c_b,
    halves, gram, coef, strip_coef, start, after_one, edges, weights,
    wraps_of, state, later, flux, slope, field_slope, grid_state, total,
):
    fields, count, rows, _ = probes.shape
    grid = Grid(rows)
    groups = count // 8
    tall, first, bottom = grid.tall, grid.first, grid.bottom
    even_x = lax.rem(lax.axis_index("gx"), 2) == 0
    weights[...] = difference_weights()

    def x_before(i):
        return jnp.where(even_x, x_b[i], x_a[i])

    def x_after(i):
        return jnp.where(even_x, x_a[i], x_b[i])

    base = fields * count
    coef[:, grid.own] = coef_in[:, grid.own]
    fold(coef, first, HALO, [x_before(base + a) for a in range(4)])
    fold(coef, bottom, HALO, [x_after(base + a) for a in range(4)])
    strip_coef[:, grid.own] = strip_coef_in[:, grid.own]
    start[:, :, pl.ds(TOP, 16)] = start_in[:, :, pl.ds(TOP, 16)]
    start[:, :, pl.ds(bottom - 16, 16)] = start_in[:, :, pl.ds(bottom - 16, 16)]
    for at in grid.middle:
        after_one[:, :, pl.ds(at, 8)] = after_one_in[:, :, pl.ds(at, 8)]
    blank = jnp.zeros((8 - HALO, LANES), jnp.float32)

    def corner(k, c, before):
        value = jnp.where(even_x == before, c_b[k, c], c_a[k, c])
        return jnp.concatenate([blank, value] if before else [value, blank], 0)

    unpack(0, 8, lambda k, c: corner(k, c, True), strip_coef, start, fields, groups)
    unpack(bottom, 8, lambda k, c: corner(k, c, False), strip_coef, start, fields, groups)

    def strip_body(g, carry):
        mine = flux.at[0]
        strip_velocities(grid.outer, grid.outer, g, start, after_one, strip_coef, mine, edges, 0)
        for at in grid.beside_outer:
            here = pl.ds(at, 8)
            mine[0, here] = strip_coef[0, here] * after_one[1, g, here]
        strip_heights(grid.outer, g, after_one, strip_coef, mine)
        strip_velocities(grid.tiles, [], g, after_one, None, strip_coef, mine, edges, 4, lack=SECOND)
        return carry

    lax.fori_loop(0, groups, strip_body, 0)
    near = 16

    def body(i, carry):
        for k in range(WIDE):
            p = WIDE * i + k
            for c in range(fields):
                for at in (0, rows - near):
                    sea = coef[3, pl.ds(TOP + at, near)] != 0.0
                    value = probes[c, p, pl.ds(at, near)].astype(jnp.float32)
                    state[k, c, pl.ds(TOP + at, near)] = jnp.where(sea, value, 0.0)
                state[k, c, pl.ds(first, HALO)] = x_before(c * count + p)
                state[k, c, pl.ds(bottom, HALO)] = x_after(c * count + p)
                later[k, c, pl.ds(grid.middle[0], 8 * len(grid.middle))] = inner[p, c]
            for slot in range(4 * STEPS):
                for at in grid.outer if slot < 4 else grid.tiles:
                    here = pl.ds(at, 8)
                    wraps_of[k, slot, here] = pltpu.roll(edges[slot, p // 8, here], turn_of(p), 1)

        for k in range(WIDE):

            def write_velocity(at, e_new, n_new):
                if at in grid.outer:
                    later[k, 1, pl.ds(at, 8)] = e_new
                    later[k, 2, pl.ds(at, 8)] = n_new

            def write_height(at, h_new):
                later[k, 0, pl.ds(at, 8)] = h_new

            def across(at):
                value, lane = flux[k, 1, pl.ds(at, 8)], lane_ids(8)
                up = jnp.where(lane == LANES - 1, 0.0, pltpu.roll(value, LANES - 1, 1))
                down = jnp.where(lane == 0, 0.0, pltpu.roll(value, 1, 1))
                return up - down + jnp.where(ends(), wraps_of[k, 3, pl.ds(at, 8)], 0.0)

            for at in grid.beside_outer:
                here = pl.ds(at, 8)
                flux[k, 0, here] = coef[0, here] * later[k, 1, here]
            velocities(
                grid.outer, lambda c: state.at[k, c], coef,
                lambda c, at, value: shifted(value, wraps_of[k, c, pl.ds(at, 8)]),
                flux.at[k], write_velocity,
            )
            heights(grid.outer, coef, across, flux.at[k], write_height)

        field_products(grid, later, field_slope, weights, SECOND)
        for k in range(WIDE):

            def differences(c, at, value):
                wrap = wraps_of[k, 4 + c, pl.ds(at, 8)]
                if c not in SECOND:
                    return shifted(value, wrap)
                known = field_slope[SECOND.index(c), pl.ds(k * grid.padded + at - first, 8)]
                return known + jnp.where(ends(), wrap, 0.0)

            def row(c):
                return pl.multiple_of((c * count + WIDE * i + k) * tall, 8)

            def write_velocity(at, e_new, n_new):
                grid_state[pl.ds(row(1) + (at - first), 8)] = e_new
                grid_state[pl.ds(row(2) + (at - first), 8)] = n_new

            velocities(
                grid.tiles, lambda c: later.at[k, c], coef,
                differences, flux.at[k], write_velocity,
            )
        flux_products(grid, flux, slope, weights)
        for k in range(WIDE):

            def row(c):
                return pl.multiple_of((c * count + WIDE * i + k) * tall, 8)

            def write_height(at, h_new):
                grid_state[pl.ds(row(0) + (at - first), 8)] = h_new

            def across(at):
                wrap = wraps_of[k, 7, pl.ds(at, 8)]
                return slope[pl.ds(k * grid.padded + at - first, 8)] + jnp.where(ends(), wrap, 0.0)

            heights(grid.tiles, coef, across, flux.at[k], write_height)
        return carry

    lax.fori_loop(0, count // WIDE, body, 0)

    total[...] = jnp.zeros_like(total)

    def gram_body(i, acc):
        c, block = i // (rows // BLOCK), lax.rem(i, rows // BLOCK)
        at = c * count * tall + block * BLOCK + HALO
        values = jnp.concatenate(
            [grid_state[pl.ds(at + x, count, stride=tall)] for x in range(BLOCK)], 1
        )
        top = values.astype(jnp.bfloat16)
        low = (values - top.astype(jnp.float32)).astype(jnp.bfloat16)
        both = jnp.concatenate([top, low], 0)
        halves[i] = both
        return acc + lax.dot_general(
            both, both, (((1,), (1,)), ((), ())), preferred_element_type=jnp.float32
        )

    acc = jnp.zeros((2 * count, 2 * count), jnp.float32)
    acc = lax.fori_loop(0, fields * rows // BLOCK, gram_body, acc, unroll=True)
    total[:, : 2 * count] = acc
    value = total[...]
    summed = value[:count] + value[count:]
    summed = summed + pltpu.roll(summed, LANES - count, 1)
    lane = lane_ids(count)
    summed = jnp.where(lane < count, summed, 0.0)
    out = summed[:8]
    for b in range(1, count // 8):
        out = out + pltpu.roll(summed[8 * b : 8 * b + 8], count * b, 1)
    gram[...] = out


def evolve(probes, known, *received):
    fields, count, rows, cols = probes.shape
    grid = Grid(rows)
    f32, groups, height = jnp.float32, count // 8, grid.height
    return pl.pallas_call(
        evolve_kernel,
        out_shape=(
            jax.ShapeDtypeStruct((fields * rows // BLOCK, 2 * count, BLOCK * cols), jnp.bfloat16),
            jax.ShapeDtypeStruct((8, LANES), f32),
        ),
        scratch_shapes=[
            pltpu.VMEM((4, height, LANES), f32),
            pltpu.VMEM((4, height, LANES), f32),
            pltpu.VMEM((fields, groups, height, LANES), f32),
            pltpu.VMEM((fields, groups, height, LANES), f32),
            pltpu.VMEM((4 * STEPS, groups, height, LANES), f32),
            pltpu.VMEM((2 * LANES, LANES), jnp.bfloat16),
            pltpu.VMEM((WIDE, 4 * STEPS, height, LANES), f32),
            pltpu.VMEM((WIDE, fields, height, LANES), f32),
            pltpu.VMEM((WIDE, fields, height, LANES), f32),
            pltpu.VMEM((WIDE, 3, height, LANES), f32),
            pltpu.VMEM((WIDE * grid.padded, LANES), f32),
            pltpu.VMEM((max(len(SECOND), 1), WIDE * grid.padded, LANES), f32),
            pltpu.VMEM((fields * count * grid.tall, LANES), f32),
            pltpu.VMEM((2 * count, LANES), f32),
        ],
        compiler_params=pltpu.CompilerParams(vmem_limit_bytes=30 * MIB),
        cost_estimate=pl.CostEstimate(flops=10**8, bytes_accessed=10**7, transcendentals=0),
        name="evolve_and_gram",
    )(probes, *known, *received)


def finish_kernel(scale, grams, halves, basis, triangle, grid_out, staged, sems):
    fields, count, rows, cols = staged.shape
    stride = grid_out.shape[0] // count
    summed = jnp.sum(grams[...], 0)
    lane = lane_ids(count)
    row_id = lax.broadcasted_iota(jnp.int32, (count, LANES), 0)
    gram = jnp.concatenate(
        [summed if b == 0 else pltpu.roll(summed, LANES - count * b, 1) for b in range(count // 8)],
        0,
    )
    work = jnp.where(lane < count, gram, jnp.where(lane == row_id + count, 1.0, 0.0))
    part = [work[8 * i : 8 * i + 8] for i in range(count // 8)]
    row8 = lax.broadcasted_iota(jnp.int32, (8, LANES), 0)

    def spread(value, k):
        return jnp.broadcast_to(value[:, k : k + 1], (8, LANES))

    for k in range(0, count, PIVOTS):
        span = range(PIVOTS)
        block = part[k // 8]
        pivot_rows = [jnp.broadcast_to(block[k % 8 + i : k % 8 + i + 1], (8, LANES)) for i in span]
        inner = [[spread(pivot_rows[j], k + i) for i in span] for j in span]
        columns = {r: [spread(part[r], k + i) for i in span] for r in range(k // 8, count // 8)}
        inverses = []
        for i in span:
            inverses.append(1.0 / inner[i][i])
            for j in range(i + 1, PIVOTS):
                ratio = inner[j][i] * inverses[i]
                pivot_rows[j] = pivot_rows[j] - ratio * pivot_rows[i]
                for m in range(i + 1, PIVOTS):
                    inner[j][m] = inner[j][m] - ratio * inner[i][m]
        for r, column in columns.items():
            ratios = []
            for i in span:
                left = column[i]
                for m in range(i):
                    left = left - ratios[m] * inner[m][i]
                left = left * inverses[i]
                if r == k // 8:
                    left = jnp.where(row8 > k % 8 + i, left, 0.0)
                ratios.append(left)
            for i in span:
                part[r] = part[r] - ratios[i] * pivot_rows[i]
    work = jnp.concatenate(part, 0)
    pivots = jnp.sum(jnp.where(lane == row_id, work, 0.0), 1, keepdims=True)
    work = work / jnp.sqrt(pivots)
    triangle[...] = jnp.where(lane >= row_id, work, 0.0)[:, :count] * (1.0 / scale)
    lower = (work * scale)[:, count : 2 * count]
    top = lower.astype(jnp.bfloat16)
    low = (lower - top.astype(jnp.float32)).astype(jnp.bfloat16)
    factor = jnp.concatenate([top, top, low], 1)

    copies = []
    for c in range(fields):

        def body(i, carry):
            both = halves[c * (rows // BLOCK) + i]
            stacked = jnp.concatenate([both, both[:count]], 0)
            out = jnp.dot(factor, stacked, preferred_element_type=jnp.float32)
            for x in range(BLOCK):
                at = BLOCK * i + x
                grid_out[pl.ds(at, count, stride=stride)] = out[:, x * cols : (x + 1) * cols]
            return carry

        lax.fori_loop(0, rows // BLOCK, body, 0, unroll=True)

        for part_of in range(PARTS):
            these = pl.ds(part_of * count // PARTS, count // PARTS)

            def store(q, carry):
                q = q + part_of * count // PARTS
                at = pl.multiple_of(q * stride, 8)
                staged[c, q] = grid_out[pl.ds(at, rows)].astype(jnp.bfloat16)
                return carry

            lax.fori_loop(0, count // PARTS, store, 0, unroll=4)
            copies.append(
                pltpu.make_async_copy(
                    staged.at[c, these], basis.at[c, these], sems.at[c * PARTS + part_of]
                )
            )
            copies[-1].start()
    for copy in copies:
        copy.wait()


def finish(grams, halves, shape, scale):
    fields, count, rows, cols = shape
    return pl.pallas_call(
        functools.partial(finish_kernel, scale),
        out_shape=(
            jax.ShapeDtypeStruct(shape, jnp.bfloat16),
            jax.ShapeDtypeStruct((count, count), jnp.float32),
        ),
        out_specs=(
            pl.BlockSpec(memory_space=pltpu.HBM),
            pl.BlockSpec(memory_space=pltpu.VMEM),
        ),
        scratch_shapes=[
            pltpu.VMEM((count * (rows + 8), cols), jnp.float32),
            pltpu.VMEM(shape, jnp.bfloat16),
            pltpu.SemaphoreType.DMA((fields * PARTS,)),
        ],
        compiler_params=pltpu.CompilerParams(vmem_limit_bytes=20 * MIB),
        name="factor_and_apply",
    )(grams, halves)


def first_pairs(size):
    return [(i, i ^ 1) for i in range(size)]


def second_pairs(size):
    return [(i, ((i + 1) ^ 1) - 1) for i in range(1, size - 1)]


def per_device(probes, depth, east_flow, north_flow, land_sea):
    fields, count, rows, cols = probes.shape
    nx, ny = lax.axis_size("gx"), lax.axis_size("gy")
    coefs = (depth, east_flow, north_flow, land_sea)
    x_a, x_b, to_a, to_b, held = pack(probes, *coefs)
    from_b = lax.ppermute(to_b, "gy", second_pairs(ny))
    from_a = lax.ppermute(to_a, "gy", first_pairs(ny))
    got_xb = lax.ppermute(x_b, "gx", second_pairs(nx))
    got_xa = lax.ppermute(x_a, "gx", first_pairs(nx))
    *firsts, coef = alone(held, coefs)
    low_high = corners((to_a, to_b, from_a, from_b), firsts[0])
    c_b = lax.ppermute(low_high[1], "gx", second_pairs(nx))
    c_a = lax.ppermute(low_high[0], "gx", first_pairs(nx))
    inner, *strip_arrays = middle(firsts, coef, to_a, to_b, from_a, from_b)
    halves, gram = evolve(held, (inner, coef, *strip_arrays), got_xa, got_xb, c_a, c_b)
    devices = nx * ny
    grams = lax.all_to_all(
        jnp.broadcast_to(gram[None], (devices,) + gram.shape), ("gx", "gy"), 0, 0
    )
    scale = math.sqrt(fields * rows * nx * cols * ny)
    return finish(grams, halves, probes.shape, scale)


def solution(mesh):
    in_specs = (
        P(None, None, "gx", "gy"),
        P("gx", "gy"),
        P("gx", "gy"),
        P("gx", "gy"),
        P("gx", "gy"),
    )
    out_specs = (P(None, None, "gx", "gy"), P())
    return jax.shard_map(
        per_device, mesh=mesh, in_specs=in_specs, out_specs=out_specs, check_vma=False
    )
```

```python
import functools
import math

import jax
import jax.numpy as jnp
from jax import lax
from jax.experimental import pallas as pl
from jax.experimental.pallas import tpu as pltpu
from jax.sharding import PartitionSpec as P

STEPS = 2
HALO = 2 * STEPS
LANES = 128
TOP = 8

time_step = 0.3
coriolis = 0.5
gravity = 1.0

MIB = 1024 * 1024
BLOCK = 8
PARTS = 1
FIRST = (0, 1)
SECOND = (0, 1, 2)
PIVOTS = 8
WIDE = 8


def lane_ids(rows):
    return lax.broadcasted_iota(jnp.int32, (rows, LANES), 1)


def in_hbm(arrays):
    return [pltpu.with_memory_space_constraint(v, pltpu.HBM) for v in arrays]


def pack_kernel(
    probes, depth, east_flow, north_flow, land_sea,
    x_a, x_b, y_a, y_b, held, coefs, mask, sems,
):
    fields, count, rows, _ = held.shape
    even_x = lax.rem(lax.axis_index("gx"), 2) == 0
    even_y = lax.rem(lax.axis_index("gy"), 2) == 0
    small = [
        pltpu.make_async_copy(source, target, sems.at[fields + i])
        for i, (source, target) in enumerate(
            ((land_sea, mask), (depth, coefs.at[0]), (east_flow, coefs.at[1]), (north_flow, coefs.at[2]))
        )
    ]
    large = [
        pltpu.make_async_copy(probes.at[c], held.at[c], sems.at[c]) for c in range(fields)
    ]
    for copy in small + large:
        copy.start()
    for copy in small:
        copy.wait()
    lane = lane_ids(rows)
    coefs[3] = mask[...].astype(jnp.float32)

    def place(index, low, high, value):
        at = HALO * index
        turned = pltpu.roll(value, at, 1) if index else value
        low = jnp.where((lane >= at) & (lane < at + HALO), turned, low)
        back = (at - HALO) % LANES
        high = jnp.where((lane >= back) & (lane < back + HALO), turned, high)
        return low, high

    def rows_out(at, value):
        low, high = value[:HALO], value[rows - HALO :]
        x_a[at] = jnp.where(even_x, high, low)
        x_b[at] = jnp.where(even_x, low, high)

    def columns_out(at, low, high):
        y_a[at] = jnp.where(even_y, high, low)
        y_b[at] = jnp.where(even_y, low, high)

    zero = jnp.zeros((rows, LANES), jnp.float32)
    low, high = zero, zero
    for a in range(4):
        value = coefs[a]
        rows_out(fields * count + a, value)
        low, high = place(a, low, high, value)
    columns_out(fields, low, high)
    for c in range(fields):
        large[c].wait()
        low, high = zero, zero
        for p in range(count):
            value = held[c, p].astype(jnp.float32) * coefs[3]
            rows_out(c * count + p, value)
            low, high = place(p, low, high, value)
        columns_out(c, low, high)


def pack(*arguments):
    probes = arguments[0]
    fields, count, rows, cols = probes.shape
    f32 = jnp.float32
    x_shape = jax.ShapeDtypeStruct((fields * count + 4, HALO, cols), f32)
    y_shape = jax.ShapeDtypeStruct((fields + 1, rows, LANES), f32)
    return pl.pallas_call(
        pack_kernel,
        in_specs=[pl.BlockSpec(memory_space=pltpu.HBM)] * 5,
        out_shape=(
            x_shape, x_shape, y_shape, y_shape,
            jax.ShapeDtypeStruct(probes.shape, probes.dtype),
        ),
        scratch_shapes=[
            pltpu.VMEM((4, rows, cols), f32),
            pltpu.VMEM((rows, cols), jnp.int32),
            pltpu.SemaphoreType.DMA((fields + 4,)),
        ],
        compiler_params=pltpu.CompilerParams(vmem_limit_bytes=16 * MIB),
        name="pack_edges",
    )(*in_hbm(arguments))


class Grid:
    def __init__(self, rows):
        self.rows = rows
        self.own = pl.ds(TOP, rows)
        self.bottom = TOP + rows
        self.first = TOP - HALO
        self.tall = rows + 2 * HALO
        self.tiles = [self.first + 8 * t for t in range(self.tall // 8)]
        self.padded = 16 * ((self.tall + 15) // 16)
        self.window = pl.ds(self.first, self.padded)
        self.height = self.padded + TOP
        self.middle = self.tiles[1:-1]
        self.outer = [self.tiles[0], self.tiles[-1]]
        self.beside_outer = [self.tiles[1], self.tiles[-2]]


def fold(out, at, size, values):
    deep, east, north, sea = values
    half = 0.5 * time_step
    out[0, pl.ds(at, size)] = deep
    out[1, pl.ds(at, size)] = half * sea * east
    out[2, pl.ds(at, size)] = half * sea * north
    out[3, pl.ds(at, size)] = (half * gravity) * sea


def unpack(at, size, tile_of, strip_coef, strips, fields, groups):
    back = (HALO, 0, HALO, 0)
    lane = lane_ids(size)
    part = lax.rem(lane, 16) // HALO

    def gathered(plane, slot):
        out = None
        for k in range(4):
            index = (HALO * slot + lax.rem(lane, HALO) - back[k] + LANES) & (LANES - 1)
            picked = jnp.take_along_axis(tile_of(k, plane), index, axis=1)
            out = picked if out is None else jnp.where(part == k, picked, out)
        return out

    fold(strip_coef, at, size, [gathered(fields, jnp.full_like(lane, a)) for a in range(4)])
    for c in range(fields):
        for g in range(groups):
            strips[c, g, pl.ds(at, size)] = gathered(c, 8 * g + lane // 16)


def two(value):
    top = value.astype(jnp.bfloat16)
    return top, (value - top.astype(jnp.float32)).astype(jnp.bfloat16)


def shifted(value, wrap):
    lane = lane_ids(8)
    up = value if wrap is None else jnp.where(lane == 0, wrap, value)
    down = value if wrap is None else jnp.where(lane == LANES - 1, wrap, value)
    return pltpu.roll(up, LANES - 1, 1) - pltpu.roll(down, 1, 1)


def ends():
    lane = lane_ids(8)
    return (lane == 0) | (lane == LANES - 1)


def velocities(tiles, source, factors, differences, flux, write):
    for at in tiles:
        here, above, below = pl.ds(at, 8), pl.ds(at - 1, 8), pl.ds(at + 1, 8)
        deep, east, north, slope = [factors[a, here] for a in range(4)]
        h, e, n = [source(c)[here] for c in range(3)]
        xh, xe, xn = [source(c)[below] - source(c)[above] for c in range(3)]
        yh, ye, yn = [differences(c, at, v) for c, v in enumerate((h, e, n))]
        e_new = e + (time_step * coriolis) * n - (east * xe + north * ye + slope * xh)
        n_new = n - (time_step * coriolis) * e - (east * xn + north * yn + slope * yh)
        flux[0, here] = deep * e_new
        flux[1, here] = deep * n_new
        flux[2, here] = h - (east * xh + north * yh)
        write(at, e_new, n_new)


def heights(tiles, factors, across, flux, write):
    for at in tiles:
        here, above, below = pl.ds(at, 8), pl.ds(at - 1, 8), pl.ds(at + 1, 8)
        along = flux[0, below] - flux[0, above]
        write(at, flux[2, here] - factors[3, here] * (along + across(at)))


def plain(c, at, value):
    return shifted(value, None)


def keep(edges, slot, g, at, value):
    here = lax.rem(lane_ids(8), 16) == HALO
    edges[slot, g, pl.ds(at, 8)] = jnp.where(here, pltpu.roll(value, LANES - 8, 1), value)


def keep_flux(edges, slot, g, at, value):
    edges[slot, g, pl.ds(at, 8)] = lacking(value)


def lacking(value):
    here = lax.rem(lane_ids(8), 16) == HALO
    return jnp.where(here, -pltpu.roll(value, 1, 1), pltpu.roll(value, LANES - 9, 1))


def beside(value):
    here = lax.rem(lane_ids(8), 16) == HALO
    return jnp.where(here, value, pltpu.roll(value, LANES - 8, 1))


def keep_lacking(edges, g, at, now, strip_coef):
    here = pl.ds(at, 8)
    north, slope = beside(strip_coef[2, here]), beside(strip_coef[3, here])
    h, e, n = [lacking(now[c, g, here]) for c in range(3)]
    edges[0, g, here] = -north * h
    edges[1, g, here] = -north * e
    edges[2, g, here] = -(north * n + slope * h)


def strip_velocities(tiles, written, g, now, later, strip_coef, flux, edges, slot, alone=False, lack=()):
    for at in tiles:
        if alone:
            keep_lacking(edges, g, at, now, strip_coef)
            continue
        for c in range(3):
            save = keep_flux if c in lack else keep
            save(edges, slot + c, g, at, now[c, g, pl.ds(at, 8)])

    def write(at, e_new, n_new):
        if later is not None and at in written:
            later[1, g, pl.ds(at, 8)] = e_new
            later[2, g, pl.ds(at, 8)] = n_new

    velocities(tiles, lambda c: now.at[c, g], strip_coef, plain, flux, write)
    for at in tiles:
        keep_flux(edges, slot + 3, g, at, flux[1, pl.ds(at, 8)])


def strip_heights(tiles, g, later, strip_coef, flux):
    def write(at, h_new):
        later[0, g, pl.ds(at, 8)] = h_new

    heights(tiles, strip_coef, lambda at: shifted(flux[1, pl.ds(at, 8)], None), flux, write)


def difference_weights():
    source = lax.broadcasted_iota(jnp.int32, (2 * LANES, LANES), 0) & (LANES - 1)
    target = lax.broadcasted_iota(jnp.int32, (2 * LANES, LANES), 1)
    plus = (source == target + 1).astype(jnp.float32)
    minus = (source == target - 1).astype(jnp.float32)
    return (plus - minus).astype(jnp.bfloat16)


def field_products(grid, source, slope, weights, chosen):
    for j, c in enumerate(chosen):
        for k in range(WIDE):
            slope[j, k * grid.padded : (k + 1) * grid.padded] = jnp.dot(
                jnp.concatenate(two(source[k, c, grid.window]), 1),
                weights[...],
                preferred_element_type=jnp.float32,
            )


def flux_products(grid, flux, slope, weights):
    for k in range(WIDE):
        slope[k * grid.padded : (k + 1) * grid.padded] = jnp.dot(
            jnp.concatenate(two(flux[k, 1, grid.window]), 1),
            weights[...],
            preferred_element_type=jnp.float32,
        )


def turn_of(p):
    return lax.rem(2 * LANES - 16 * lax.rem(p, 8) - HALO, LANES)


def alone_kernel(
    probes, depth, east_flow, north_flow, land_sea, first_e, first_n, first_h, coef,
    raw, mask, state, flux, slope, weights, sems,
):
    fields, count, rows, _ = probes.shape
    grid = Grid(rows)
    copies = [
        pltpu.make_async_copy(source, target, sems.at[i])
        for i, (source, target) in enumerate(
            ((land_sea, mask), (depth, raw.at[0]), (east_flow, raw.at[1]), (north_flow, raw.at[2]))
        )
    ]
    for copy in copies:
        copy.start()
    for copy in copies:
        copy.wait()
    raw[3] = mask[...].astype(jnp.float32)
    fold(coef, TOP, rows, [raw[a] for a in range(4)])
    lane = lane_ids(8)
    weights[...] = difference_weights()[:LANES]

    def differences(k, c, at, value):
        if c in FIRST:
            return slope[FIRST.index(c), pl.ds(k * grid.padded + at - grid.first, 8)]
        up = jnp.where(lane == LANES - 1, 0.0, pltpu.roll(value, LANES - 1, 1))
        return up - jnp.where(lane == 0, 0.0, pltpu.roll(value, 1, 1))

    def body(i, carry):
        for k in range(WIDE):
            p = WIDE * i + k
            for c in range(fields):
                state[k, c, grid.own] = probes[c, p].astype(jnp.float32) * raw[3]
        for j, c in enumerate(FIRST):
            for k in range(WIDE):
                slope[j, k * grid.padded : (k + 1) * grid.padded] = jnp.dot(
                    state[k, c, grid.window].astype(jnp.bfloat16),
                    weights[...],
                    preferred_element_type=jnp.float32,
                )
        for k in range(WIDE):
            p = WIDE * i + k

            def write(at, e_new, n_new):
                first_e[p, pl.ds(at - grid.first, 8)] = e_new
                first_n[p, pl.ds(at - grid.first, 8)] = n_new
                first_h[p, pl.ds(at - grid.first, 8)] = flux[k, 2, pl.ds(at, 8)]

            velocities(
                grid.tiles, lambda c: state.at[k, c], coef,
                functools.partial(differences, k), flux.at[k], write,
            )
        return carry

    lax.fori_loop(0, count // WIDE, body, 0)


def alone(probes, arguments):
    fields, count, rows, cols = probes.shape
    grid = Grid(rows)
    f32, height = jnp.float32, grid.height
    vmem, hbm = pl.BlockSpec(memory_space=pltpu.VMEM), pl.BlockSpec(memory_space=pltpu.HBM)
    one = jax.ShapeDtypeStruct((count, grid.tall, LANES), f32)
    return pl.pallas_call(
        alone_kernel,
        in_specs=[vmem] + [hbm] * 4,
        out_shape=(one, one, one, jax.ShapeDtypeStruct((4, height, LANES), f32)),
        scratch_shapes=[
            pltpu.VMEM((4, rows, cols), f32),
            pltpu.VMEM((rows, cols), jnp.int32),
            pltpu.VMEM((WIDE, fields, height, LANES), f32),
            pltpu.VMEM((WIDE, 3, height, LANES), f32),
            pltpu.VMEM((max(len(FIRST), 1), WIDE * grid.padded, LANES), f32),
            pltpu.VMEM((LANES, LANES), jnp.bfloat16),
            pltpu.SemaphoreType.DMA((4,)),
        ],
        compiler_params=pltpu.CompilerParams(vmem_limit_bytes=20 * MIB),
        cost_estimate=pl.CostEstimate(flops=10**8, bytes_accessed=10**7, transcendentals=0),
        name="first_velocities",
    )(probes, *in_hbm(arguments))


def corner_kernel(to_a, to_b, from_a, from_b, unused, c_a, c_b):
    planes, rows, _ = to_a.shape
    even_x = lax.rem(lax.axis_index("gx"), 2) == 0
    even_y = lax.rem(lax.axis_index("gy"), 2) == 0
    for k, (yes, no) in enumerate(((from_b, from_a), (to_b, to_a), (to_a, to_b), (from_a, from_b))):
        for c in range(planes):
            low = jnp.where(even_y, yes[c, pl.ds(0, HALO)], no[c, pl.ds(0, HALO)])
            end = pl.ds(rows - HALO, HALO)
            high = jnp.where(even_y, yes[c, end], no[c, end])
            c_a[k, c] = jnp.where(even_x, high, low)
            c_b[k, c] = jnp.where(even_x, low, high)


def corners(edges, before):
    shape = jax.ShapeDtypeStruct((4, edges[0].shape[0], HALO, LANES), jnp.float32)
    vmem, anywhere = pl.BlockSpec(memory_space=pltpu.VMEM), pl.BlockSpec(memory_space=pl.ANY)
    return pl.pallas_call(
        corner_kernel,
        in_specs=[vmem] * 4 + [anywhere],
        out_shape=(shape, shape),
        compiler_params=pltpu.CompilerParams(vmem_limit_bytes=8 * MIB),
        name="corner_rows",
    )(*edges, before)


def middle_kernel(
    first_e, first_n, first_h, coef, to_a, to_b, from_a, from_b,
    inner, strip_coef, start, after_one,
    edges, weights, wraps_of, flux, slope,
):
    count, fields = first_e.shape[0], to_a.shape[0] - 1
    rows = to_a.shape[1]
    grid = Grid(rows)
    groups = count // 8
    weights[...] = difference_weights()
    even_y = lax.rem(lax.axis_index("gy"), 2) == 0

    def kinds(k, *at):
        mine, theirs = (to_b, to_a) if k in (1, 2) else (from_b, from_a)
        if k in (2, 3):
            mine, theirs = theirs, mine
        return jnp.where(even_y, mine[at], theirs[at])

    for t in range(rows // 8):
        unpack(
            TOP + 8 * t, 8, lambda k, c: kinds(k, c, pl.ds(8 * t, 8)), strip_coef, start, fields, groups
        )

    def strip_body(g, carry):
        strip_velocities(
            grid.tiles, grid.middle, g, start, after_one, strip_coef, flux.at[0], edges, 0, True
        )
        strip_heights(grid.middle, g, after_one, strip_coef, flux.at[0])
        return carry

    lax.fori_loop(0, groups, strip_body, 0)

    def body(i, carry):
        for k in range(WIDE):
            p = WIDE * i + k
            for slot in range(4):
                for at in grid.tiles:
                    here = pl.ds(at, 8)
                    wraps_of[k, slot, here] = pltpu.roll(edges[slot, p // 8, here], turn_of(p), 1)
        for k in range(WIDE):
            p = WIDE * i + k
            for at in grid.tiles:
                here, there = pl.ds(at, 8), pl.ds(at - grid.first, 8)
                h, e, n = [
                    first[p, there] + jnp.where(ends(), wraps_of[k, c, here], 0.0)
                    for c, first in enumerate((first_h, first_e, first_n))
                ]
                deep = coef[0, here]
                flux[k, 0, here] = deep * e
                flux[k, 1, here] = deep * n
                flux[k, 2, here] = h
                if at in grid.middle:
                    inner[p, 1, pl.ds(at - grid.middle[0], 8)] = e
                    inner[p, 2, pl.ds(at - grid.middle[0], 8)] = n
        flux_products(grid, flux, slope, weights)
        for k in range(WIDE):
            p = WIDE * i + k

            def write_height(at, h_new):
                inner[p, 0, pl.ds(at - grid.middle[0], 8)] = h_new

            def across(at):
                wrap = wraps_of[k, 3, pl.ds(at, 8)]
                known = slope[pl.ds(k * grid.padded + at - grid.first, 8)]
                return known + jnp.where(ends(), wrap, 0.0)

            heights(grid.middle, coef, across, flux.at[k], write_height)
        return carry

    lax.fori_loop(0, count // WIDE, body, 0)


def middle(firsts, coef, *edges):
    fields, rows = edges[0].shape[0] - 1, edges[0].shape[1]
    count = firsts[0].shape[0]
    grid = Grid(rows)
    f32, groups, height = jnp.float32, count // 8, grid.height
    full = jax.ShapeDtypeStruct((fields, groups, height, LANES), f32)
    return pl.pallas_call(
        middle_kernel,
        out_shape=(
            jax.ShapeDtypeStruct((count, fields, 8 * len(grid.middle), LANES), f32),
            jax.ShapeDtypeStruct((4, height, LANES), f32),
            full,
            full,
        ),
        scratch_shapes=[
            pltpu.VMEM((4, groups, height, LANES), f32),
            pltpu.VMEM((2 * LANES, LANES), jnp.bfloat16),
            pltpu.VMEM((WIDE, 4, height, LANES), f32),
            pltpu.VMEM((WIDE, 3, height, LANES), f32),
            pltpu.VMEM((WIDE * grid.padded, LANES), f32),
        ],
        compiler_params=pltpu.CompilerParams(vmem_limit_bytes=24 * MIB),
        cost_estimate=pl.CostEstimate(flops=10**8, bytes_accessed=10**7, transcendentals=0),
        name="first_step",
    )(*firsts, coef, *edges)


def evolve_kernel(
    probes, inner, coef_in, strip_coef_in, start_in, after_one_in, x_a, x_b, c_a, c_b,
    halves, gram, coef, strip_coef, start, after_one, edges, weights,
    wraps_of, state, later, flux, slope, field_slope, grid_state, total,
):
    fields, count, rows, _ = probes.shape
    grid = Grid(rows)
    groups = count // 8
    tall, first, bottom = grid.tall, grid.first, grid.bottom
    even_x = lax.rem(lax.axis_index("gx"), 2) == 0
    weights[...] = difference_weights()

    def x_before(i):
        return jnp.where(even_x, x_b[i], x_a[i])

    def x_after(i):
        return jnp.where(even_x, x_a[i], x_b[i])

    base = fields * count
    coef[:, grid.own] = coef_in[:, grid.own]
    fold(coef, first, HALO, [x_before(base + a) for a in range(4)])
    fold(coef, bottom, HALO, [x_after(base + a) for a in range(4)])
    strip_coef[:, grid.own] = strip_coef_in[:, grid.own]
    start[:, :, pl.ds(TOP, 16)] = start_in[:, :, pl.ds(TOP, 16)]
    start[:, :, pl.ds(bottom - 16, 16)] = start_in[:, :, pl.ds(bottom - 16, 16)]
    for at in grid.middle:
        after_one[:, :, pl.ds(at, 8)] = after_one_in[:, :, pl.ds(at, 8)]
    blank = jnp.zeros((8 - HALO, LANES), jnp.float32)

    def corner(k, c, before):
        value = jnp.where(even_x == before, c_b[k, c], c_a[k, c])
        return jnp.concatenate([blank, value] if before else [value, blank], 0)

    unpack(0, 8, lambda k, c: corner(k, c, True), strip_coef, start, fields, groups)
    unpack(bottom, 8, lambda k, c: corner(k, c, False), strip_coef, start, fields, groups)

    def strip_body(g, carry):
        mine = flux.at[0]
        strip_velocities(grid.outer, grid.outer, g, start, after_one, strip_coef, mine, edges, 0)
        for at in grid.beside_outer:
            here = pl.ds(at, 8)
            mine[0, here] = strip_coef[0, here] * after_one[1, g, here]
        strip_heights(grid.outer, g, after_one, strip_coef, mine)
        strip_velocities(grid.tiles, [], g, after_one, None, strip_coef, mine, edges, 4, lack=SECOND)
        return carry

    lax.fori_loop(0, groups, strip_body, 0)
    near = 16

    def body(i, carry):
        for k in range(WIDE):
            p = WIDE * i + k
            for c in range(fields):
                for at in (0, rows - near):
                    sea = coef[3, pl.ds(TOP + at, near)] != 0.0
                    value = probes[c, p, pl.ds(at, near)].astype(jnp.float32)
                    state[k, c, pl.ds(TOP + at, near)] = jnp.where(sea, value, 0.0)
                state[k, c, pl.ds(first, HALO)] = x_before(c * count + p)
                state[k, c, pl.ds(bottom, HALO)] = x_after(c * count + p)
                later[k, c, pl.ds(grid.middle[0], 8 * len(grid.middle))] = inner[p, c]
            for slot in range(4 * STEPS):
                for at in grid.outer if slot < 4 else grid.tiles:
                    here = pl.ds(at, 8)
                    wraps_of[k, slot, here] = pltpu.roll(edges[slot, p // 8, here], turn_of(p), 1)

        for k in range(WIDE):

            def write_velocity(at, e_new, n_new):
                if at in grid.outer:
                    later[k, 1, pl.ds(at, 8)] = e_new
                    later[k, 2, pl.ds(at, 8)] = n_new

            def write_height(at, h_new):
                later[k, 0, pl.ds(at, 8)] = h_new

            def across(at):
                value, lane = flux[k, 1, pl.ds(at, 8)], lane_ids(8)
                up = jnp.where(lane == LANES - 1, 0.0, pltpu.roll(value, LANES - 1, 1))
                down = jnp.where(lane == 0, 0.0, pltpu.roll(value, 1, 1))
                return up - down + jnp.where(ends(), wraps_of[k, 3, pl.ds(at, 8)], 0.0)

            for at in grid.beside_outer:
                here = pl.ds(at, 8)
                flux[k, 0, here] = coef[0, here] * later[k, 1, here]
            velocities(
                grid.outer, lambda c: state.at[k, c], coef,
                lambda c, at, value: shifted(value, wraps_of[k, c, pl.ds(at, 8)]),
                flux.at[k], write_velocity,
            )
            heights(grid.outer, coef, across, flux.at[k], write_height)

        field_products(grid, later, field_slope, weights, SECOND)
        for k in range(WIDE):

            def differences(c, at, value):
                wrap = wraps_of[k, 4 + c, pl.ds(at, 8)]
                if c not in SECOND:
                    return shifted(value, wrap)
                known = field_slope[SECOND.index(c), pl.ds(k * grid.padded + at - first, 8)]
                return known + jnp.where(ends(), wrap, 0.0)

            def row(c):
                return pl.multiple_of((c * count + WIDE * i + k) * tall, 8)

            def write_velocity(at, e_new, n_new):
                grid_state[pl.ds(row(1) + (at - first), 8)] = e_new
                grid_state[pl.ds(row(2) + (at - first), 8)] = n_new

            velocities(
                grid.tiles, lambda c: later.at[k, c], coef,
                differences, flux.at[k], write_velocity,
            )
        flux_products(grid, flux, slope, weights)
        for k in range(WIDE):

            def row(c):
                return pl.multiple_of((c * count + WIDE * i + k) * tall, 8)

            def write_height(at, h_new):
                grid_state[pl.ds(row(0) + (at - first), 8)] = h_new

            def across(at):
                wrap = wraps_of[k, 7, pl.ds(at, 8)]
                return slope[pl.ds(k * grid.padded + at - first, 8)] + jnp.where(ends(), wrap, 0.0)

            heights(grid.tiles, coef, across, flux.at[k], write_height)
        return carry

    lax.fori_loop(0, count // WIDE, body, 0)

    total[...] = jnp.zeros_like(total)

    def gram_body(i, acc):
        c, block = i // (rows // BLOCK), lax.rem(i, rows // BLOCK)
        at = c * count * tall + block * BLOCK + HALO
        values = jnp.concatenate(
            [grid_state[pl.ds(at + x, count, stride=tall)] for x in range(BLOCK)], 1
        )
        top = values.astype(jnp.bfloat16)
        low = (values - top.astype(jnp.float32)).astype(jnp.bfloat16)
        both = jnp.concatenate([top, low], 0)
        halves[i] = both
        return acc + lax.dot_general(
            both, both, (((1,), (1,)), ((), ())), preferred_element_type=jnp.float32
        )

    acc = jnp.zeros((2 * count, 2 * count), jnp.float32)
    acc = lax.fori_loop(0, fields * rows // BLOCK, gram_body, acc, unroll=True)
    total[:, : 2 * count] = acc
    value = total[...]
    summed = value[:count] + value[count:]
    summed = summed + pltpu.roll(summed, LANES - count, 1)
    lane = lane_ids(count)
    summed = jnp.where(lane < count, summed, 0.0)
    out = summed[:8]
    for b in range(1, count // 8):
        out = out + pltpu.roll(summed[8 * b : 8 * b + 8], count * b, 1)
    gram[...] = out


def evolve(probes, known, *received):
    fields, count, rows, cols = probes.shape
    grid = Grid(rows)
    f32, groups, height = jnp.float32, count // 8, grid.height
    return pl.pallas_call(
        evolve_kernel,
        out_shape=(
            jax.ShapeDtypeStruct((fields * rows // BLOCK, 2 * count, BLOCK * cols), jnp.bfloat16),
            jax.ShapeDtypeStruct((8, LANES), f32),
        ),
        scratch_shapes=[
            pltpu.VMEM((4, height, LANES), f32),
            pltpu.VMEM((4, height, LANES), f32),
            pltpu.VMEM((fields, groups, height, LANES), f32),
            pltpu.VMEM((fields, groups, height, LANES), f32),
            pltpu.VMEM((4 * STEPS, groups, height, LANES), f32),
            pltpu.VMEM((2 * LANES, LANES), jnp.bfloat16),
            pltpu.VMEM((WIDE, 4 * STEPS, height, LANES), f32),
            pltpu.VMEM((WIDE, fields, height, LANES), f32),
            pltpu.VMEM((WIDE, fields, height, LANES), f32),
            pltpu.VMEM((WIDE, 3, height, LANES), f32),
            pltpu.VMEM((WIDE * grid.padded, LANES), f32),
            pltpu.VMEM((max(len(SECOND), 1), WIDE * grid.padded, LANES), f32),
            pltpu.VMEM((fields * count * grid.tall, LANES), f32),
            pltpu.VMEM((2 * count, LANES), f32),
        ],
        compiler_params=pltpu.CompilerParams(vmem_limit_bytes=30 * MIB),
        cost_estimate=pl.CostEstimate(flops=10**8, bytes_accessed=10**7, transcendentals=0),
        name="evolve_and_gram",
    )(probes, *known, *received)


def finish_kernel(scale, grams, halves, basis, triangle, grid_out, staged, sems):
    fields, count, rows, cols = staged.shape
    stride = grid_out.shape[0] // count
    summed = jnp.sum(grams[...], 0)
    lane = lane_ids(count)
    row_id = lax.broadcasted_iota(jnp.int32, (count, LANES), 0)
    gram = jnp.concatenate(
        [summed if b == 0 else pltpu.roll(summed, LANES - count * b, 1) for b in range(count // 8)],
        0,
    )
    work = jnp.where(lane < count, gram, jnp.where(lane == row_id + count, 1.0, 0.0))
    part = [work[8 * i : 8 * i + 8] for i in range(count // 8)]
    row8 = lax.broadcasted_iota(jnp.int32, (8, LANES), 0)

    def spread(value, k):
        return jnp.broadcast_to(value[:, k : k + 1], (8, LANES))

    for k in range(0, count, PIVOTS):
        span = range(PIVOTS)
        block = part[k // 8]
        pivot_rows = [jnp.broadcast_to(block[k % 8 + i : k % 8 + i + 1], (8, LANES)) for i in span]
        inner = [[spread(pivot_rows[j], k + i) for i in span] for j in span]
        columns = {r: [spread(part[r], k + i) for i in span] for r in range(k // 8, count // 8)}
        inverses = []
        for i in span:
            inverses.append(1.0 / inner[i][i])
            for j in range(i + 1, PIVOTS):
                ratio = inner[j][i] * inverses[i]
                pivot_rows[j] = pivot_rows[j] - ratio * pivot_rows[i]
                for m in range(i + 1, PIVOTS):
                    inner[j][m] = inner[j][m] - ratio * inner[i][m]
        for r, column in columns.items():
            ratios = []
            for i in span:
                left = column[i]
                for m in range(i):
                    left = left - ratios[m] * inner[m][i]
                left = left * inverses[i]
                if r == k // 8:
                    left = jnp.where(row8 > k % 8 + i, left, 0.0)
                ratios.append(left)
            for i in span:
                part[r] = part[r] - ratios[i] * pivot_rows[i]
    work = jnp.concatenate(part, 0)
    pivots = jnp.sum(jnp.where(lane == row_id, work, 0.0), 1, keepdims=True)
    work = work / jnp.sqrt(pivots)
    triangle[...] = jnp.where(lane >= row_id, work, 0.0)[:, :count] * (1.0 / scale)
    lower = (work * scale)[:, count : 2 * count]
    top = lower.astype(jnp.bfloat16)
    low = (lower - top.astype(jnp.float32)).astype(jnp.bfloat16)
    factor = jnp.concatenate([top, top, low], 1)

    copies = []
    for c in range(fields):

        def body(i, carry):
            both = halves[c * (rows // BLOCK) + i]
            stacked = jnp.concatenate([both, both[:count]], 0)
            out = jnp.dot(factor, stacked, preferred_element_type=jnp.float32)
            for x in range(BLOCK):
                at = BLOCK * i + x
                grid_out[pl.ds(at, count, stride=stride)] = out[:, x * cols : (x + 1) * cols]
            return carry

        lax.fori_loop(0, rows // BLOCK, body, 0, unroll=True)

        for part_of in range(PARTS):
            these = pl.ds(part_of * count // PARTS, count // PARTS)

            def store(q, carry):
                q = q + part_of * count // PARTS
                at = pl.multiple_of(q * stride, 8)
                staged[c, q] = grid_out[pl.ds(at, rows)].astype(jnp.bfloat16)
                return carry

            lax.fori_loop(0, count // PARTS, store, 0, unroll=True)
            copies.append(
                pltpu.make_async_copy(
                    staged.at[c, these], basis.at[c, these], sems.at[c * PARTS + part_of]
                )
            )
            copies[-1].start()
    for copy in copies:
        copy.wait()


def finish(grams, halves, shape, scale):
    fields, count, rows, cols = shape
    return pl.pallas_call(
        functools.partial(finish_kernel, scale),
        out_shape=(
            jax.ShapeDtypeStruct(shape, jnp.bfloat16),
            jax.ShapeDtypeStruct((count, count), jnp.float32),
        ),
        out_specs=(
            pl.BlockSpec(memory_space=pltpu.HBM),
            pl.BlockSpec(memory_space=pltpu.VMEM),
        ),
        scratch_shapes=[
            pltpu.VMEM((count * (rows + 8), cols), jnp.float32),
            pltpu.VMEM(shape, jnp.bfloat16),
            pltpu.SemaphoreType.DMA((fields * PARTS,)),
        ],
        compiler_params=pltpu.CompilerParams(vmem_limit_bytes=20 * MIB),
        name="factor_and_apply",
    )(grams, halves)


def first_pairs(size):
    return [(i, i ^ 1) for i in range(size)]


def second_pairs(size):
    return [(i, ((i + 1) ^ 1) - 1) for i in range(1, size - 1)]


def per_device(probes, depth, east_flow, north_flow, land_sea):
    fields, count, rows, cols = probes.shape
    nx, ny = lax.axis_size("gx"), lax.axis_size("gy")
    coefs = (depth, east_flow, north_flow, land_sea)
    x_a, x_b, to_a, to_b, held = pack(probes, *coefs)
    from_b = lax.ppermute(to_b, "gy", second_pairs(ny))
    from_a = lax.ppermute(to_a, "gy", first_pairs(ny))
    got_xb = lax.ppermute(x_b, "gx", second_pairs(nx))
    got_xa = lax.ppermute(x_a, "gx", first_pairs(nx))
    *firsts, coef = alone(held, coefs)
    low_high = corners((to_a, to_b, from_a, from_b), firsts[0])
    c_b = lax.ppermute(low_high[1], "gx", second_pairs(nx))
    c_a = lax.ppermute(low_high[0], "gx", first_pairs(nx))
    inner, *strip_arrays = middle(firsts, coef, to_a, to_b, from_a, from_b)
    halves, gram = evolve(held, (inner, coef, *strip_arrays), got_xa, got_xb, c_a, c_b)
    devices = nx * ny
    grams = lax.all_to_all(
        jnp.broadcast_to(gram[None], (devices,) + gram.shape), ("gx", "gy"), 0, 0
    )
    scale = math.sqrt(fields * rows * nx * cols * ny)
    return finish(grams, halves, probes.shape, scale)


def solution(mesh):
    in_specs = (
        P(None, None, "gx", "gy"),
        P("gx", "gy"),
        P("gx", "gy"),
        P("gx", "gy"),
        P("gx", "gy"),
    )
    out_specs = (P(None, None, "gx", "gy"), P())
    return jax.shard_map(
        per_device, mesh=mesh, in_specs=in_specs, out_specs=out_specs, check_vma=False
    )
```
